512 devices in a mesh: chrom: 32 (over x, z), genome: 16 (over y, core).
Axes of the slice: x: 4, y: 8, z: 8, core: 2. Of those that a mesh axis runs over, the one named last changes fastest.
Arguments:
- panel: bfloat16 [768, 262144], P(None, ('chrom', 'genome')), may hold values from -30 to 30
- zscores: float32 [262144], P(('chrom', 'genome')), may hold values from -40 to 40
- block_chrom: int32 [512], P(('chrom', 'genome')), may hold values from 0 to 511, as said below
- lr_partner: int32 [512, 2], P(('chrom', 'genome')), may hold values from 0 to 511, as said below
Outputs:
- whitened: float32 [262144], P(('chrom', 'genome'))
- enrichment: float32 [32], P('chrom')
The draws below stay inside these ranges and needn't reach their ends.
Inputs may be any that keep to these rules, and one draw needn't show every extreme that they name: `block_chrom`: chromosome numbers never fall along the blocks of one group of 16 blocks, and no two groups share a number. `lr_partner`: each entry names a block of the same group of 16 blocks other than the block itself.
All inputs are finite; a program needn't handle non-finite values.
Results may differ from the reference program's by a relative error of at most 0.0003.
Values may be sent and summed in bfloat16 or wider, within the bound.
No kernel may reach another device: no remote copies, remote signals or barrier semaphores. Data moves between devices by JAX's collectives and lax.ppermute only.
A program may use at most 64 MiB of HBM per device.

```python
import jax
import jax.numpy as jnp
from jax import lax

BLOCK = 512
SAMPLES = 768
LONG_PAIRS = 2
NS_ITERS = 3
GROUP = 16
NBLOCKS = 512


def draw_panel(key, part):
    key = jax.random.fold_in(key, 11)
    key_base, key_scale = jax.random.split(key)
    base_draw = jnp.clip(jax.random.normal(key_base, (SAMPLES, NBLOCKS * BLOCK), jnp.float32), -6.0, 6.0)
    scales = jnp.exp(jax.random.uniform(key_scale, (NBLOCKS * BLOCK,), jnp.float32, -1.15, 1.15))
    return (base_draw * scales[None, :]).astype(jnp.bfloat16)


def draw_zscores(key, part):
    key = jax.random.fold_in(key, 23)
    variant_index = jnp.arange(NBLOCKS * BLOCK, dtype=jnp.int32)
    block_of = variant_index // BLOCK
    position = (block_of % GROUP).astype(jnp.float32)
    group_of = (block_of // GROUP).astype(jnp.float32)
    groups_all = NBLOCKS // GROUP
    rising = (1.0 + 2.0 * position / (GROUP - 1)) * (1.0 + group_of / max(groups_all - 1, 1))
    base_draw = jnp.clip(jax.random.normal(key, (NBLOCKS * BLOCK,), jnp.float32), -6.0, 6.0)
    return base_draw * rising


def draw_block_chrom(key, part):
    key = jax.random.fold_in(key, 37)
    flags = (jax.random.randint(key, (NBLOCKS,), 0, 3) == 0).astype(jnp.int32)
    position = jnp.arange(NBLOCKS, dtype=jnp.int32) % GROUP
    flags = jnp.where(position == 0, 0, flags)
    within = jnp.cumsum(flags.reshape(NBLOCKS // GROUP, GROUP), axis=1)
    slack = GROUP - 1 - within[:, GROUP - 1:GROUP]
    group_rows = jnp.arange(NBLOCKS // GROUP, dtype=jnp.int32)[:, None]
    lifted = within + jnp.where(group_rows == NBLOCKS // GROUP - 1, slack, 0)
    return (group_rows * GROUP + lifted).reshape(-1).astype(jnp.int32)


def draw_lr_partner(key, part):
    key = jax.random.fold_in(key, 53)
    block_of = jnp.arange(NBLOCKS, dtype=jnp.int32)[:, None]
    offsets = jax.random.randint(key, (NBLOCKS, LONG_PAIRS), 1, GROUP)
    offsets = offsets.at[2, 0].set(GROUP - 1)
    offsets = offsets.at[NBLOCKS - 3, 0].set(1)
    offsets = offsets.at[5, 1].set(GROUP // 2)
    position = (block_of % GROUP + offsets) % GROUP
    return (block_of // GROUP * GROUP + position).astype(jnp.int32)


def setup_inputs(seed: int = 0) -> dict:
    streams_of = jax.random.split(jax.random.key(seed), 5)
    return {
        "panel": draw_panel(jax.random.fold_in(streams_of[4], 71), 0),
        "zscores": draw_zscores(jax.random.fold_in(streams_of[4], 71), 0),
        "block_chrom": draw_block_chrom(jax.random.fold_in(streams_of[4], 71), 0),
        "lr_partner": draw_lr_partner(jax.random.fold_in(streams_of[4], 71), 0),
    }


ridge_term = 0.5
leak_weight = 0.25

def exact_dot(left_mat, right_mat):
    return jnp.dot(left_mat, right_mat, precision=lax.Precision.HIGHEST)

def inverse_root(matrix):
    fro_scale = jnp.sqrt(jnp.sum(matrix * matrix) + 1e-06)
    normed = matrix / fro_scale
    identity = jnp.eye(BLOCK, dtype=jnp.float32)
    iterate = identity
    for step_index in range(NS_ITERS):
        square = exact_dot(iterate, iterate)
        product = exact_dot(square, normed)
        iterate = 0.5 * exact_dot(iterate, 3.0 * identity - product)
    return iterate

def reference(panel, zscores, block_chrom, lr_partner):
    columns = panel.astype(jnp.float32).reshape(SAMPLES, NBLOCKS, BLOCK)
    z_blocks = zscores.reshape(NBLOCKS, BLOCK)

    def cross_ld(own_block, other_index):
        other_block = lax.dynamic_index_in_dim(columns, other_index, 1, keepdims=False)
        rounded = (exact_dot(own_block.T, other_block) / SAMPLES).astype(jnp.bfloat16)
        rounded = lax.optimization_barrier(rounded)
        return rounded.astype(jnp.float32)

    def one_block(block_index):
        own_block = lax.dynamic_index_in_dim(columns, block_index, 1, keepdims=False)
        position = block_index % GROUP
        left_index = jnp.maximum(block_index - 1, 0).astype(jnp.int32)
        right_index = jnp.minimum(block_index + 1, NBLOCKS - 1).astype(jnp.int32)
        left_flag = ((position != 0) & (block_chrom[left_index] == block_chrom[block_index])).astype(jnp.float32)
        right_flag = ((position != GROUP - 1) & (block_chrom[right_index] == block_chrom[block_index])).astype(jnp.float32)
        partner_list = [(left_index, left_flag), (right_index, right_flag)]
        for pair_index in range(LONG_PAIRS):
            partner_list.append((lr_partner[block_index, pair_index].astype(jnp.int32), jnp.float32(1.0)))
        leakage = jnp.zeros((BLOCK, BLOCK), jnp.float32)
        for partner_index, weight_flag in partner_list:
            crossed = cross_ld(own_block, partner_index) * weight_flag
            leakage = leakage + exact_dot(crossed, crossed.T)
        local_ld = exact_dot(own_block.T, own_block) / SAMPLES + ridge_term * jnp.eye(BLOCK, dtype=jnp.float32) + leak_weight * leakage
        inverse_sqrt = inverse_root(local_ld)
        z_block = lax.dynamic_index_in_dim(z_blocks, block_index, 0, keepdims=False)
        return exact_dot(inverse_sqrt, z_block)
    whitened = lax.map(one_block, jnp.arange(NBLOCKS, dtype=jnp.int32)).reshape(-1)
    group_sums = lax.optimization_barrier(jnp.sum((whitened * whitened).reshape(NBLOCKS // GROUP, GROUP * BLOCK), axis=1))
    enrichment = group_sums * (NBLOCKS // GROUP) / jnp.sum(group_sums)
    return (whitened, enrichment)
```

```python
import functools

import jax
import jax.numpy as jnp
from jax import lax
from jax.experimental import pallas as pl
from jax.experimental.pallas import tpu as pltpu
from jax.sharding import PartitionSpec as P

ridge_term = 0.5
leak_weight = 0.25

TILE = 128
SUB = 16
META_P0, META_P1, META_HI, META_LO = 3, 4, 5, 6

NT = (((1,), (1,)), ((), ()))
VMEM = pl.BlockSpec(memory_space=pltpu.VMEM)
SMEM = pl.BlockSpec(memory_space=pltpu.SMEM)


def tile_order(tiles):
    below = [(i, j) for j in range(tiles) for i in range(j + 1, tiles)]
    return below + [(2 * c, 2 * c) for c in range(tiles // 2)]


def grid_ids(shape):
    return lax.broadcasted_iota(jnp.int32, shape, 0), lax.broadcasted_iota(jnp.int32, shape, 1)


def pieces(start, share):
    out, row = [], 0
    while row < TILE:
        owner, place = divmod(start + row, share)
        length = min(TILE - row, share - place)
        out.append((row, owner, place, length))
        row += length
    return out


def gram_kernel(owners, share, partner_ref, chrom_ref, panel_ref, out_ref):
    samples = panel_ref.shape[0]
    tiles = samples // TILE
    order = {tile: n for n, tile in enumerate(tile_order(tiles))}
    rows, cols = grid_ids((TILE, TILE))
    metas = []

    def put(tile, value):
        value = value.astype(jnp.bfloat16)
        for row, owner, place, length in pieces(order[tile] * TILE, share):
            out_ref[owner, place : place + length, :] = value[row : row + length, :]

    for c in range(tiles // 2):
        low = 2 * c * TILE
        product = lax.dot_general(
            panel_ref[low:, :], panel_ref[low : low + 2 * TILE, :], NT, preferred_element_type=jnp.float32
        )
        for j in (2 * c, 2 * c + 1):
            for i in range(j + 1, tiles):
                put((i, j), product[i * TILE - low : (i + 1) * TILE - low, (j - 2 * c) * TILE : (j - 2 * c + 1) * TILE])
        first, second = product[:TILE, :TILE], product[TILE : 2 * TILE, TILE:]
        halved = jnp.where(rows == cols, 0.5 * second, second)
        put((2 * c, 2 * c), jnp.where(rows > cols, first, halved))
        metas.append(jnp.sum(jnp.where(rows == cols, 0.5 * first, 0.0), axis=0, keepdims=True))

    owner_rows, _ = grid_ids((SUB, TILE))
    meta = jnp.zeros((SUB, TILE), jnp.float32)
    for n, diagonal in enumerate(metas):
        meta = jnp.where(owner_rows == n, diagonal, meta)
    chrom = chrom_ref[0]
    for n, number in (
        (META_P0, lax.rem(partner_ref[0, 0], owners)),
        (META_P1, lax.rem(partner_ref[0, 1], owners)),
        (META_HI, chrom // 16),
        (META_LO, lax.rem(chrom, 16)),
    ):
        meta = jnp.where(owner_rows == n, number.astype(jnp.float32), meta)
    meta = meta.astype(jnp.bfloat16)
    for owner in range(owners):
        out_ref[owner, share : share + SUB, :] = meta


def mix_kernel(in_ref, out_ref):
    owners, height, _ = in_ref.shape
    meta = in_ref[:, height - SUB :, :].astype(jnp.float32)

    def spread(n):
        return jnp.broadcast_to(meta[:, n : n + 1, :], (owners, SUB, TILE))

    def flat(value):
        return value.reshape(owners * SUB, TILE)

    high, low = spread(META_HI), spread(META_LO)
    same = jnp.where(
        (high[1:] == high[:-1]) & (low[1:] == low[:-1]), 1.0, 0.0
    )
    edge = jnp.zeros((1, SUB, TILE), jnp.float32)
    with_right = flat(jnp.concatenate([same, edge], axis=0))
    with_left = flat(jnp.concatenate([edge, same], axis=0))
    first, second = flat(spread(META_P0)), flat(spread(META_P1))
    rows, cols = grid_ids((owners * SUB, TILE))
    own = (rows // SUB).astype(jnp.float32)
    halves = []
    for h in range(owners * SUB // TILE):
        other = (cols // SUB + h * (TILE // SUB)).astype(jnp.float32)
        count = jnp.where(first == other, 1.0, 0.0) + jnp.where(second == other, 1.0, 0.0)
        count = count + jnp.where(own + 1.0 == other, with_right, 0.0) + jnp.where(own - 1.0 == other, with_left, 0.0)
        halves.append(jnp.where(rows % SUB == cols % SUB, count, 0.0))
    weights = jnp.concatenate(halves, axis=1).astype(jnp.bfloat16)

    groups = height // SUB
    for g in range(0, groups, 2):
        members = list(range(g, min(g + 2, groups)))
        stacked = jnp.concatenate(
            [in_ref[:, m * SUB : (m + 1) * SUB, :].reshape(owners * SUB, TILE) for m in members], axis=1
        )
        mixed = jnp.dot(weights, stacked, preferred_element_type=jnp.float32).astype(jnp.bfloat16)
        for n, m in enumerate(members):
            out_ref[:, m * SUB : (m + 1) * SUB, :] = mixed[:, n * TILE : (n + 1) * TILE].reshape(owners, SUB, TILE)


def finish_kernel(share, sums_ref, columns_ref, base_ref, z_ref, out_ref, total_ref, half, scaled, first_iterate):
    samples = columns_ref.shape[1]
    width = columns_ref.shape[0]
    tiles = samples // TILE
    order = {tile: n for n, tile in enumerate(tile_order(tiles))}
    rows, cols = grid_ids((TILE, TILE))
    zero = jnp.zeros((TILE, TILE), jnp.bfloat16)

    def get(tile):
        return jnp.concatenate(
            [
                sums_ref[owner, place : place + length, :]
                for _, owner, place, length in pieces(order[tile] * TILE, share)
            ],
            axis=0,
        )

    def place(i, j, value):
        half[i * TILE : (i + 1) * TILE, j * TILE : (j + 1) * TILE] = value

    meta = sums_ref[0, share : share + SUB, :].astype(jnp.float32)
    for c in range(tiles // 2):
        for j in (2 * c, 2 * c + 1):
            for i in range(j + 1, tiles):
                place(i, j, get((i, j)))
        packed = get((2 * c, 2 * c)).astype(jnp.float32)
        lower = jnp.where(rows > cols, packed, jnp.where(rows == cols, meta[c : c + 1, :], 0.0))
        place(2 * c, 2 * c, lower.astype(jnp.bfloat16))
        place(2 * c + 1, 2 * c + 1, jnp.where(rows <= cols, packed, 0.0).astype(jnp.bfloat16))
        place(2 * c, 2 * c + 1, zero)

    scale = leak_weight / (samples * samples)
    columns = columns_ref[...]
    parts = []
    for c in range(tiles // 2):
        top = (2 * c + 2) * TILE
        parts.append(
            lax.dot_general(
                columns[:, :top], half[2 * c * TILE : top, :top], NT, preferred_element_type=jnp.float32
            )
            * scale
        )
    turned = jnp.concatenate(parts, axis=1).astype(jnp.bfloat16)
    matrix = (
        base_ref[...]
        + lax.dot_general(columns, turned, NT, preferred_element_type=jnp.float32)
        + lax.dot_general(turned, columns, NT, preferred_element_type=jnp.float32)
    )
    norm = jnp.sqrt(jnp.sum(matrix * matrix, keepdims=True) + 1e-06)
    matrix = matrix / norm
    scaled[...] = matrix
    wide_rows, wide_cols = grid_ids((width, width))
    first_iterate[...] = jnp.where(wide_rows == wide_cols, 1.5, 0.0) - 0.5 * matrix

    eye = rows == cols
    blocks = width // TILE

    def to_column(ref, row):
        return jnp.sum(ref[...] * row, axis=1, keepdims=True)

    def to_row(ref, column):
        return jnp.sum(ref[...] * column, axis=0, keepdims=True)

    def turned_column(column):
        return jnp.concatenate(
            [
                jnp.sum(jnp.where(eye, column[n * TILE : (n + 1) * TILE], 0.0), axis=0, keepdims=True)
                for n in range(blocks)
            ],
            axis=1,
        )

    def turned_row(row):
        return jnp.concatenate(
            [
                jnp.sum(jnp.where(eye, row[:, n * TILE : (n + 1) * TILE], 0.0), axis=1, keepdims=True)
                for n in range(blocks)
            ],
            axis=0,
        )

    def second_iterate(column):
        inner = to_row(scaled, column)
        inner = to_column(first_iterate, inner)
        inner = to_row(first_iterate, inner)
        return 0.5 * to_column(first_iterate, 3.0 * turned_column(column) - inner)

    z_row = z_ref[...]
    product = second_iterate(second_iterate(to_column(scaled, z_row)))
    answer = 0.5 * second_iterate(3.0 * turned_row(z_row) - product)
    answer = turned_column(answer)
    out_ref[...] = answer
    total_ref[...] = jnp.broadcast_to(jnp.sum(answer * answer, keepdims=True).reshape(1, 1, 1), total_ref.shape)


def local(panel, zscores, block_chrom, lr_partner):
    samples, width = panel.shape
    owners = lax.axis_size("genome")
    chroms = lax.axis_size("chrom")
    tiles = samples // TILE
    share = len(tile_order(tiles)) * TILE // owners
    packed_shape = jax.ShapeDtypeStruct((owners, share + SUB, TILE), jnp.bfloat16)
    params = pltpu.CompilerParams(vmem_limit_bytes=48 * 2**20)

    packed = pl.pallas_call(
        functools.partial(gram_kernel, owners, share),
        out_shape=packed_shape,
        in_specs=[SMEM, SMEM, VMEM],
        out_specs=VMEM,
        compiler_params=params,
    )(lr_partner, block_chrom, panel)
    held = lax.all_to_all(packed, "genome", 0, 0, tiled=True)

    mixed = pl.pallas_call(
        mix_kernel,
        out_shape=packed_shape,
        in_specs=[VMEM],
        out_specs=VMEM,
        compiler_params=params,
    )(held)
    sums = lax.all_to_all(mixed, "genome", 0, 0, tiled=True)

    columns = panel.T
    base = lax.dot_general(
        panel, panel, (((0,), (0,)), ((), ())), preferred_element_type=jnp.float32
    ) * (1.0 / samples) + ridge_term * jnp.eye(width, dtype=jnp.float32)

    whitened, totals = pl.pallas_call(
        functools.partial(finish_kernel, share),
        out_shape=(
            jax.ShapeDtypeStruct((1, width), jnp.float32),
            jax.ShapeDtypeStruct((owners, 1, TILE), jnp.float32),
        ),
        in_specs=[VMEM] * 4,
        out_specs=(VMEM, VMEM),
        scratch_shapes=[
            pltpu.VMEM((samples, samples), jnp.bfloat16),
            pltpu.VMEM((width, width), jnp.float32),
            pltpu.VMEM((width, width), jnp.float32),
        ],
        compiler_params=params,
    )(sums, columns, base, zscores.reshape(1, width))

    of_group = lax.all_to_all(totals, "genome", 0, 0, tiled=True)
    group_sum = jnp.sum(of_group, axis=0).reshape(TILE)[:chroms]
    of_all = lax.all_to_all(group_sum, "chrom", 0, 0, tiled=True)
    enrichment = group_sum[:1] * chroms / jnp.sum(of_all)
    return (whitened.reshape(width), enrichment)


def solution(mesh):
    placed = (
        P(None, ("chrom", "genome")),
        P(("chrom", "genome")),
        P(("chrom", "genome")),
        P(("chrom", "genome"), None),
    )
    return jax.shard_map(
        local,
        mesh=mesh,
        in_specs=placed,
        out_specs=(P(("chrom", "genome")), P("chrom")),
        check_vma=False,
    )
```

```python
import functools

import jax
import jax.numpy as jnp
from jax import lax
from jax.experimental import pallas as pl
from jax.experimental.pallas import tpu as pltpu
from jax.sharding import PartitionSpec as P

ridge_term = 0.5
leak_weight = 0.25

TILE = 128
SUB = 16
META = 8
META_P0, META_P1, META_HI, META_LO = 3, 4, 5, 6

NT = (((1,), (1,)), ((), ()))
VMEM = pl.BlockSpec(memory_space=pltpu.VMEM)
HBM = pl.BlockSpec(memory_space=pltpu.HBM)
SMEM = pl.BlockSpec(memory_space=pltpu.SMEM)


def tile_order(tiles):
    below = [(i, j) for j in range(tiles) for i in range(j + 1, tiles)]
    return below + [(2 * c, 2 * c) for c in range(tiles // 2)]


def grid_ids(shape):
    return lax.broadcasted_iota(jnp.int32, shape, 0), lax.broadcasted_iota(jnp.int32, shape, 1)


def pieces(start, share):
    out, row = [], 0
    while row < TILE:
        owner, place = divmod(start + row, share)
        length = min(TILE - row, share - place)
        out.append((row, owner, place, length))
        row += length
    return out


def gram_kernel(owners, share, partner_hbm, chrom_ref, panel_hbm, out_ref, panel_ref, partner_ref, sems):
    samples = panel_ref.shape[0]
    tiles = samples // TILE
    bands = tiles // 2
    arriving = []
    for c in reversed(range(bands)):
        band = pl.ds(2 * c * TILE, 2 * TILE)
        arriving.append(pltpu.make_async_copy(panel_hbm.at[band], panel_ref.at[band], sems.at[c]))
    small = [
        pltpu.make_async_copy(partner_hbm, partner_ref, sems.at[bands]),
    ]
    for copy in arriving + small:
        copy.start()
    order = {tile: n for n, tile in enumerate(tile_order(tiles))}
    rows, cols = grid_ids((TILE, TILE))
    metas = []

    def put(tile, value):
        value = value.astype(jnp.bfloat16)
        for row, owner, place, length in pieces(order[tile] * TILE, share):
            out_ref[owner, place : place + length, :] = value[row : row + length, :]

    for c in reversed(range(bands)):
        arriving[bands - 1 - c].wait()
        low = 2 * c * TILE
        product = lax.dot_general(
            panel_ref[low:, :], panel_ref[low : low + 2 * TILE, :], NT, preferred_element_type=jnp.float32
        )
        for j in (2 * c, 2 * c + 1):
            for i in range(j + 1, tiles):
                put((i, j), product[i * TILE - low : (i + 1) * TILE - low, (j - 2 * c) * TILE : (j - 2 * c + 1) * TILE])
        first, second = product[:TILE, :TILE], product[TILE : 2 * TILE, TILE:]
        halved = jnp.where(rows == cols, 0.5 * second, second)
        put((2 * c, 2 * c), jnp.where(rows > cols, first, halved))
        metas.append((c, jnp.sum(jnp.where(rows == cols, 0.5 * first, 0.0), axis=0, keepdims=True)))

    owner_rows, _ = grid_ids((META, TILE))
    meta = jnp.zeros((META, TILE), jnp.float32)
    for n, diagonal in metas:
        meta = jnp.where(owner_rows == n, diagonal, meta)
    for copy in small:
        copy.wait()
    chrom = chrom_ref[0]
    for n, number in (
        (META_P0, lax.rem(partner_ref[0, 0], owners)),
        (META_P1, lax.rem(partner_ref[0, 1], owners)),
        (META_HI, chrom >> 4),
        (META_LO, chrom & 15),
    ):
        meta = jnp.where(owner_rows == n, number.astype(jnp.float32), meta)
    meta = meta.astype(jnp.bfloat16)
    for owner in range(owners):
        out_ref[owner, share : share + META, :] = meta


def mix_kernel(in_ref, out_ref):
    owners, height, _ = in_ref.shape
    share = height - META
    meta = in_ref[:, share:, :].astype(jnp.float32)

    def spread(n):
        return jnp.broadcast_to(meta[:, n : n + 1, :], (owners, SUB, TILE))

    def flat(value):
        return value.reshape(owners * SUB, TILE)

    high, low = spread(META_HI), spread(META_LO)
    same = jnp.where(
        (high[1:] == high[:-1]) & (low[1:] == low[:-1]), 1.0, 0.0
    )
    edge = jnp.zeros((1, SUB, TILE), jnp.float32)
    with_right = flat(jnp.concatenate([same, edge], axis=0))
    with_left = flat(jnp.concatenate([edge, same], axis=0))
    first, second = flat(spread(META_P0)), flat(spread(META_P1))
    rows, cols = grid_ids((owners * SUB, TILE))
    own = (rows // SUB).astype(jnp.float32)
    halves = []
    for h in range(owners * SUB // TILE):
        other = (cols // SUB + h * (TILE // SUB)).astype(jnp.float32)
        count = jnp.where(first == other, 1.0, 0.0) + jnp.where(second == other, 1.0, 0.0)
        count = count + jnp.where(own + 1.0 == other, with_right, 0.0) + jnp.where(own - 1.0 == other, with_left, 0.0)
        halves.append(jnp.where(rows % SUB == cols % SUB, count, 0.0))
    weights = jnp.concatenate(halves, axis=1).astype(jnp.bfloat16)

    groups = share // SUB
    for g in range(0, groups, 2):
        members = list(range(g, min(g + 2, groups)))
        stacked = jnp.concatenate(
            [in_ref[:, m * SUB : (m + 1) * SUB, :].reshape(owners * SUB, TILE) for m in members], axis=1
        )
        mixed = jnp.dot(weights, stacked, preferred_element_type=jnp.float32).astype(jnp.bfloat16)
        for n, m in enumerate(members):
            out_ref[:, m * SUB : (m + 1) * SUB, :] = mixed[:, n * TILE : (n + 1) * TILE].reshape(owners, SUB, TILE)
    padded = jnp.concatenate([meta, jnp.zeros((owners, SUB - META, TILE), jnp.float32)], axis=1)
    mixed = jnp.dot(
        weights, padded.reshape(owners * SUB, TILE).astype(jnp.bfloat16), preferred_element_type=jnp.float32
    )
    out_ref[:, share:, :] = mixed.reshape(owners, SUB, TILE)[:, :META, :].astype(jnp.bfloat16)


def finish_kernel(share, sums_ref, columns_ref, base_ref, z_ref, out_ref, total_ref, half, scaled, first_iterate):
    samples = columns_ref.shape[1]
    width = columns_ref.shape[0]
    tiles = samples // TILE
    order = {tile: n for n, tile in enumerate(tile_order(tiles))}
    rows, cols = grid_ids((TILE, TILE))
    zero = jnp.zeros((TILE, TILE), jnp.bfloat16)

    def get(tile):
        return jnp.concatenate(
            [
                sums_ref[owner, place : place + length, :]
                for _, owner, place, length in pieces(order[tile] * TILE, share)
            ],
            axis=0,
        )

    def place(i, j, value):
        half[i * TILE : (i + 1) * TILE, j * TILE : (j + 1) * TILE] = value

    meta = sums_ref[0, share : share + META, :].astype(jnp.float32)
    for c in range(tiles // 2):
        for j in (2 * c, 2 * c + 1):
            for i in range(j + 1, tiles):
                place(i, j, get((i, j)))
        packed = get((2 * c, 2 * c)).astype(jnp.float32)
        lower = jnp.where(rows > cols, packed, jnp.where(rows == cols, meta[c : c + 1, :], 0.0))
        place(2 * c, 2 * c, lower.astype(jnp.bfloat16))
        place(2 * c + 1, 2 * c + 1, jnp.where(rows <= cols, packed, 0.0).astype(jnp.bfloat16))
        place(2 * c, 2 * c + 1, zero)

    scale = leak_weight / (samples * samples)
    columns = columns_ref[...]
    parts = []
    for c in range(tiles // 2):
        top = (2 * c + 2) * TILE
        parts.append(
            lax.dot_general(
                columns[:, :top], half[2 * c * TILE : top, :top], NT, preferred_element_type=jnp.float32
            )
            * scale
        )
    turned = jnp.concatenate(parts, axis=1).astype(jnp.bfloat16)
    matrix = (
        base_ref[...]
        + lax.dot_general(columns, turned, NT, preferred_element_type=jnp.float32)
        + lax.dot_general(turned, columns, NT, preferred_element_type=jnp.float32)
    )
    norm = jnp.sqrt(jnp.sum(matrix * matrix, keepdims=True) + 1e-06)
    matrix = matrix / norm
    scaled[...] = matrix
    wide_rows, wide_cols = grid_ids((width, width))
    first_iterate[...] = jnp.where(wide_rows == wide_cols, 1.5, 0.0) - 0.5 * matrix

    eye = rows == cols
    blocks = width // TILE

    def to_column(ref, row):
        return jnp.sum(ref[...] * row, axis=1, keepdims=True)

    def to_row(ref, column):
        return jnp.sum(ref[...] * column, axis=0, keepdims=True)

    def turned_column(column):
        return jnp.concatenate(
            [
                jnp.sum(jnp.where(eye, column[n * TILE : (n + 1) * TILE], 0.0), axis=0, keepdims=True)
                for n in range(blocks)
            ],
            axis=1,
        )

    def turned_row(row):
        return jnp.concatenate(
            [
                jnp.sum(jnp.where(eye, row[:, n * TILE : (n + 1) * TILE], 0.0), axis=1, keepdims=True)
                for n in range(blocks)
            ],
            axis=0,
        )

    def second_iterate(column):
        inner = to_row(scaled, column)
        inner = to_column(first_iterate, inner)
        inner = to_row(first_iterate, inner)
        return 0.5 * to_column(first_iterate, 3.0 * turned_column(column) - inner)

    z_row = z_ref[...]
    product = second_iterate(second_iterate(to_column(scaled, z_row)))
    answer = 0.5 * second_iterate(3.0 * turned_row(z_row) - product)
    answer = turned_column(answer)
    out_ref[...] = answer
    total_ref[...] = jnp.broadcast_to(jnp.sum(answer * answer, keepdims=True).reshape(1, 1, 1), total_ref.shape)


def local(panel, zscores, block_chrom, lr_partner):
    samples, width = panel.shape
    owners = lax.axis_size("genome")
    chroms = lax.axis_size("chrom")
    tiles = samples // TILE
    share = len(tile_order(tiles)) * TILE // owners
    packed_shape = jax.ShapeDtypeStruct((owners, share + META, TILE), jnp.bfloat16)
    params = pltpu.CompilerParams(vmem_limit_bytes=48 * 2**20)

    lr_hbm, panel_hbm = (pltpu.with_memory_space_constraint(x, pltpu.HBM) for x in (lr_partner, panel))
    packed = pl.pallas_call(
        functools.partial(gram_kernel, owners, share),
        out_shape=packed_shape,
        in_specs=[HBM, SMEM, HBM],
        out_specs=VMEM,
        scratch_shapes=[
            pltpu.VMEM(panel.shape, panel.dtype),
            pltpu.SMEM(lr_partner.shape, jnp.int32),
            pltpu.SemaphoreType.DMA((tiles // 2 + 1,)),
        ],
        compiler_params=params,
    )(lr_hbm, block_chrom, panel_hbm)
    held = lax.all_to_all(packed, "genome", 0, 0, tiled=True)

    mixed = pl.pallas_call(
        mix_kernel,
        out_shape=packed_shape,
        in_specs=[VMEM],
        out_specs=VMEM,
        compiler_params=params,
    )(held)
    sums = lax.all_to_all(mixed, "genome", 0, 0, tiled=True)

    columns = panel.T
    base = lax.dot_general(
        panel, panel, (((0,), (0,)), ((), ())), preferred_element_type=jnp.float32
    ) * (1.0 / samples) + ridge_term * jnp.eye(width, dtype=jnp.float32)

    whitened, totals = pl.pallas_call(
        functools.partial(finish_kernel, share),
        out_shape=(
            jax.ShapeDtypeStruct((1, width), jnp.float32),
            jax.ShapeDtypeStruct((owners, 1, TILE), jnp.float32),
        ),
        in_specs=[VMEM] * 4,
        out_specs=(VMEM, VMEM),
        scratch_shapes=[
            pltpu.VMEM((samples, samples), jnp.bfloat16),
            pltpu.VMEM((width, width), jnp.float32),
            pltpu.VMEM((width, width), jnp.float32),
        ],
        compiler_params=params,
    )(sums, columns, base, zscores.reshape(1, width))

    of_group = lax.all_to_all(totals, "genome", 0, 0, tiled=True)
    group_sum = jnp.sum(of_group, axis=0, keepdims=True)
    of_all = lax.all_to_all(
        jnp.broadcast_to(group_sum, (chroms, 1, TILE)), "chrom", 0, 0, tiled=True
    )
    group_sum, of_all = lax.optimization_barrier((group_sum, of_all))
    enrichment = (group_sum * chroms / jnp.sum(of_all, axis=0, keepdims=True)).reshape(TILE)[:1]
    return (whitened.reshape(width), enrichment)


def solution(mesh):
    placed = (
        P(None, ("chrom", "genome")),
        P(("chrom", "genome")),
        P(("chrom", "genome")),
        P(("chrom", "genome"), None),
    )
    return jax.shard_map(
        local,
        mesh=mesh,
        in_specs=placed,
        out_specs=(P(("chrom", "genome")), P("chrom")),
        check_vma=False,
    )
```

```python
import functools

import jax
import jax.numpy as jnp
from jax import lax
from jax.experimental import pallas as pl
from jax.experimental.pallas import tpu as pltpu
from jax.sharding import PartitionSpec as P

ridge_term = 0.5
leak_weight = 0.25

TILE = 128
SUB = 16
META = 8
META_P0, META_P1, META_HI, META_LO = 3, 4, 5, 6

NT = (((1,), (1,)), ((), ()))
VMEM = pl.BlockSpec(memory_space=pltpu.VMEM)
HBM = pl.BlockSpec(memory_space=pltpu.HBM)
SMEM = pl.BlockSpec(memory_space=pltpu.SMEM)


def tile_order(tiles):
    below = [(i, j) for j in range(tiles) for i in range(j + 1, tiles)]
    return below + [(2 * c, 2 * c) for c in range(tiles // 2)]


def grid_ids(shape):
    return lax.broadcasted_iota(jnp.int32, shape, 0), lax.broadcasted_iota(jnp.int32, shape, 1)


def pieces(start, share):
    out, row = [], 0
    while row < TILE:
        owner, place = divmod(start + row, share)
        length = min(TILE - row, share - place)
        out.append((row, owner, place, length))
        row += length
    return out


def gram_kernel(owners, share, partner_hbm, chrom_ref, panel_hbm, out_ref, panel_ref, partner_ref, sems):
    samples = panel_ref.shape[0]
    tiles = samples // TILE
    bands = tiles // 2
    arriving = []
    for c in range(bands):
        band = pl.ds(2 * c * TILE, 2 * TILE)
        arriving.append(pltpu.make_async_copy(panel_hbm.at[band], panel_ref.at[band], sems.at[c]))
    small = [
        pltpu.make_async_copy(partner_hbm, partner_ref, sems.at[bands]),
    ]
    for copy in arriving + small:
        copy.start()
    order = {tile: n for n, tile in enumerate(tile_order(tiles))}
    rows, cols = grid_ids((TILE, TILE))
    metas = []

    def put(tile, value):
        value = value.astype(jnp.bfloat16)
        for row, owner, place, length in pieces(order[tile] * TILE, share):
            out_ref[owner, place : place + length, :] = value[row : row + length, :]

    for copy in arriving:
        copy.wait()
    for c in range(bands):
        low = 2 * c * TILE
        product = lax.dot_general(
            panel_ref[low:, :], panel_ref[low : low + 2 * TILE, :], NT, preferred_element_type=jnp.float32
        )
        for j in (2 * c, 2 * c + 1):
            for i in range(j + 1, tiles):
                put((i, j), product[i * TILE - low : (i + 1) * TILE - low, (j - 2 * c) * TILE : (j - 2 * c + 1) * TILE])
        first, second = product[:TILE, :TILE], product[TILE : 2 * TILE, TILE:]
        halved = jnp.where(rows == cols, 0.5 * second, second)
        put((2 * c, 2 * c), jnp.where(rows > cols, first, halved))
        metas.append((c, jnp.sum(jnp.where(rows == cols, 0.5 * first, 0.0), axis=0, keepdims=True)))

    owner_rows, _ = grid_ids((META, TILE))
    meta = jnp.zeros((META, TILE), jnp.float32)
    for n, diagonal in metas:
        meta = jnp.where(owner_rows == n, diagonal, meta)
    for copy in small:
        copy.wait()
    chrom = chrom_ref[0]
    for n, number in (
        (META_P0, lax.rem(partner_ref[0, 0], owners)),
        (META_P1, lax.rem(partner_ref[0, 1], owners)),
        (META_HI, chrom >> 4),
        (META_LO, chrom & 15),
    ):
        meta = jnp.where(owner_rows == n, number.astype(jnp.float32), meta)
    meta = meta.astype(jnp.bfloat16)
    for owner in range(owners):
        out_ref[owner, share : share + META, :] = meta


def mix_kernel(in_ref, out_ref):
    owners, height, _ = in_ref.shape
    share = height - META
    meta = in_ref[:, share:, :].astype(jnp.float32)

    def spread(n):
        return jnp.broadcast_to(meta[:, n : n + 1, :], (owners, SUB, TILE))

    def flat(value):
        return value.reshape(owners * SUB, TILE)

    high, low = spread(META_HI), spread(META_LO)
    same = jnp.where(
        (high[1:] == high[:-1]) & (low[1:] == low[:-1]), 1.0, 0.0
    )
    edge = jnp.zeros((1, SUB, TILE), jnp.float32)
    with_right = flat(jnp.concatenate([same, edge], axis=0))
    with_left = flat(jnp.concatenate([edge, same], axis=0))
    first, second = flat(spread(META_P0)), flat(spread(META_P1))
    rows, cols = grid_ids((owners * SUB, TILE))
    own = (rows // SUB).astype(jnp.float32)
    halves = []
    for h in range(owners * SUB // TILE):
        other = (cols // SUB + h * (TILE // SUB)).astype(jnp.float32)
        count = jnp.where(first == other, 1.0, 0.0) + jnp.where(second == other, 1.0, 0.0)
        count = count + jnp.where(own + 1.0 == other, with_right, 0.0) + jnp.where(own - 1.0 == other, with_left, 0.0)
        halves.append(jnp.where(rows % SUB == cols % SUB, count, 0.0))
    weights = jnp.concatenate(halves, axis=1).astype(jnp.bfloat16)

    groups = share // SUB
    for g in range(0, groups, 2):
        members = list(range(g, min(g + 2, groups)))
        stacked = jnp.concatenate(
            [in_ref[:, m * SUB : (m + 1) * SUB, :].reshape(owners * SUB, TILE) for m in members], axis=1
        )
        mixed = jnp.dot(weights, stacked, preferred_element_type=jnp.float32).astype(jnp.bfloat16)
        for n, m in enumerate(members):
            out_ref[:, m * SUB : (m + 1) * SUB, :] = mixed[:, n * TILE : (n + 1) * TILE].reshape(owners, SUB, TILE)
    padded = jnp.concatenate([meta, jnp.zeros((owners, SUB - META, TILE), jnp.float32)], axis=1)
    mixed = jnp.dot(
        weights, padded.reshape(owners * SUB, TILE).astype(jnp.bfloat16), preferred_element_type=jnp.float32
    )
    out_ref[:, share:, :] = mixed.reshape(owners, SUB, TILE)[:, :META, :].astype(jnp.bfloat16)


def finish_kernel(share, sums_ref, columns_ref, base_ref, z_ref, out_ref, total_ref, half, scaled, first_iterate):
    samples = columns_ref.shape[1]
    width = columns_ref.shape[0]
    tiles = samples // TILE
    order = {tile: n for n, tile in enumerate(tile_order(tiles))}
    rows, cols = grid_ids((TILE, TILE))
    zero = jnp.zeros((TILE, TILE), jnp.bfloat16)

    def get(tile):
        return jnp.concatenate(
            [
                sums_ref[owner, place : place + length, :]
                for _, owner, place, length in pieces(order[tile] * TILE, share)
            ],
            axis=0,
        )

    def place(i, j, value):
        half[i * TILE : (i + 1) * TILE, j * TILE : (j + 1) * TILE] = value

    meta = sums_ref[0, share : share + META, :].astype(jnp.float32)
    for c in range(tiles // 2):
        for j in (2 * c, 2 * c + 1):
            for i in range(j + 1, tiles):
                place(i, j, get((i, j)))
        packed = get((2 * c, 2 * c)).astype(jnp.float32)
        lower = jnp.where(rows > cols, packed, jnp.where(rows == cols, meta[c : c + 1, :], 0.0))
        place(2 * c, 2 * c, lower.astype(jnp.bfloat16))
        place(2 * c + 1, 2 * c + 1, jnp.where(rows <= cols, packed, 0.0).astype(jnp.bfloat16))
        place(2 * c, 2 * c + 1, zero)

    scale = leak_weight / (samples * samples)
    columns = columns_ref[...]
    parts = []
    for c in range(tiles // 2):
        top = (2 * c + 2) * TILE
        parts.append(
            lax.dot_general(
                columns[:, :top], half[2 * c * TILE : top, :top], NT, preferred_element_type=jnp.float32
            )
            * scale
        )
    turned = jnp.concatenate(parts, axis=1).astype(jnp.bfloat16)
    matrix = (
        base_ref[...]
        + lax.dot_general(columns, turned, NT, preferred_element_type=jnp.float32)
        + lax.dot_general(turned, columns, NT, preferred_element_type=jnp.float32)
    )
    norm = jnp.sqrt(jnp.sum(matrix * matrix, keepdims=True) + 1e-06)
    matrix = matrix / norm
    scaled[...] = matrix
    wide_rows, wide_cols = grid_ids((width, width))
    first_iterate[...] = jnp.where(wide_rows == wide_cols, 1.5, 0.0) - 0.5 * matrix

    eye = rows == cols
    blocks = width // TILE

    def to_column(ref, row):
        return jnp.sum(ref[...] * row, axis=1, keepdims=True)

    def to_row(ref, column):
        return jnp.sum(ref[...] * column, axis=0, keepdims=True)

    def turned_column(column):
        return jnp.concatenate(
            [
                jnp.sum(jnp.where(eye, column[n * TILE : (n + 1) * TILE], 0.0), axis=0, keepdims=True)
                for n in range(blocks)
            ],
            axis=1,
        )

    def turned_row(row):
        return jnp.concatenate(
            [
                jnp.sum(jnp.where(eye, row[:, n * TILE : (n + 1) * TILE], 0.0), axis=1, keepdims=True)
                for n in range(blocks)
            ],
            axis=0,
        )

    def second_iterate(column):
        inner = to_row(scaled, column)
        inner = to_column(first_iterate, inner)
        inner = to_row(first_iterate, inner)
        return 0.5 * to_column(first_iterate, 3.0 * turned_column(column) - inner)

    z_row = z_ref[...]
    product = second_iterate(second_iterate(to_column(scaled, z_row)))
    answer = 0.5 * second_iterate(3.0 * turned_row(z_row) - product)
    answer = turned_column(answer)
    out_ref[...] = answer
    total_ref[...] = jnp.broadcast_to(jnp.sum(answer * answer, keepdims=True).reshape(1, 1, 1), total_ref.shape)


def close_kernel(chroms, whitened_ref, group_ref, all_ref, out_ref, enrichment_ref):
    out_ref[...] = whitened_ref[...]
    overall = jnp.sum(all_ref[...], axis=0)
    enrichment_ref[...] = group_ref[0] * chroms / overall


def local(panel, zscores, block_chrom, lr_partner):
    samples, width = panel.shape
    owners = lax.axis_size("genome")
    chroms = lax.axis_size("chrom")
    tiles = samples // TILE
    share = len(tile_order(tiles)) * TILE // owners
    packed_shape = jax.ShapeDtypeStruct((owners, share + META, TILE), jnp.bfloat16)
    params = pltpu.CompilerParams(vmem_limit_bytes=48 * 2**20)

    lr_hbm, panel_hbm = (pltpu.with_memory_space_constraint(x, pltpu.HBM) for x in (lr_partner, panel))
    packed = pl.pallas_call(
        functools.partial(gram_kernel, owners, share),
        out_shape=packed_shape,
        in_specs=[HBM, SMEM, HBM],
        out_specs=VMEM,
        scratch_shapes=[
            pltpu.VMEM(panel.shape, panel.dtype),
            pltpu.SMEM(lr_partner.shape, jnp.int32),
            pltpu.SemaphoreType.DMA((tiles // 2 + 1,)),
        ],
        compiler_params=params,
    )(lr_hbm, block_chrom, panel_hbm)
    held = lax.all_to_all(packed, "genome", 0, 0, tiled=True)

    mixed = pl.pallas_call(
        mix_kernel,
        out_shape=packed_shape,
        in_specs=[VMEM],
        out_specs=VMEM,
        compiler_params=params,
    )(held)
    sums = lax.all_to_all(mixed, "genome", 0, 0, tiled=True)

    columns = panel.T
    base = lax.dot_general(
        panel, panel, (((0,), (0,)), ((), ())), preferred_element_type=jnp.float32
    ) * (1.0 / samples) + ridge_term * jnp.eye(width, dtype=jnp.float32)

    whitened, totals = pl.pallas_call(
        functools.partial(finish_kernel, share),
        out_shape=(
            jax.ShapeDtypeStruct((1, width), jnp.float32),
            jax.ShapeDtypeStruct((owners, 1, TILE), jnp.float32),
        ),
        in_specs=[VMEM] * 4,
        out_specs=(VMEM, VMEM),
        scratch_shapes=[
            pltpu.VMEM((samples, samples), jnp.bfloat16),
            pltpu.VMEM((width, width), jnp.float32),
            pltpu.VMEM((width, width), jnp.float32),
        ],
        compiler_params=params,
    )(sums, columns, base, zscores.reshape(1, width))

    of_group = lax.all_to_all(totals, "genome", 0, 0, tiled=True)
    group_sum = jnp.sum(of_group, axis=0, keepdims=True)
    of_all = lax.all_to_all(
        jnp.broadcast_to(group_sum, (chroms, 1, TILE)), "chrom", 0, 0, tiled=True
    )
    whitened, enrichment = pl.pallas_call(
        functools.partial(close_kernel, chroms),
        out_shape=(
            jax.ShapeDtypeStruct((1, width), jnp.float32),
            jax.ShapeDtypeStruct((1, TILE), jnp.float32),
        ),
        in_specs=[VMEM] * 3,
        out_specs=(VMEM, VMEM),
        compiler_params=params,
    )(whitened, group_sum, of_all)
    return (whitened.reshape(width), enrichment.reshape(TILE)[:1])


def solution(mesh):
    placed = (
        P(None, ("chrom", "genome")),
        P(("chrom", "genome")),
        P(("chrom", "genome")),
        P(("chrom", "genome"), None),
    )
    return jax.shard_map(
        local,
        mesh=mesh,
        in_specs=placed,
        out_specs=(P(("chrom", "genome")), P("chrom")),
        check_vma=False,
    )
```

```python
import functools

import jax
import jax.numpy as jnp
from jax import lax
from jax.experimental import pallas as pl
from jax.experimental.pallas import tpu as pltpu
from jax.sharding import PartitionSpec as P

ridge_term = 0.5
leak_weight = 0.25

TILE = 128
SUB = 16
META = 8
META_P0, META_P1, META_HI, META_LO = 3, 4, 5, 6

NT = (((1,), (1,)), ((), ()))
VMEM = pl.BlockSpec(memory_space=pltpu.VMEM)
HBM = pl.BlockSpec(memory_space=pltpu.HBM)
SMEM = pl.BlockSpec(memory_space=pltpu.SMEM)


def tile_order(tiles):
    below = [(i, j) for j in range(tiles) for i in range(j + 1, tiles)]
    return below + [(2 * c, 2 * c) for c in range(tiles // 2)]


def grid_ids(shape):
    return lax.broadcasted_iota(jnp.int32, shape, 0), lax.broadcasted_iota(jnp.int32, shape, 1)


def pieces(start, share):
    out, row = [], 0
    while row < TILE:
        owner, place = divmod(start + row, share)
        length = min(TILE - row, share - place)
        out.append((row, owner, place, length))
        row += length
    return out


def gram_kernel(owners, share, partner_hbm, chrom_ref, panel_hbm, out_ref, panel_ref, partner_ref, sems):
    samples = panel_ref.shape[0]
    tiles = samples // TILE
    bands = tiles // 2
    arriving = []
    for c in range(bands):
        band = pl.ds(2 * c * TILE, 2 * TILE)
        arriving.append(pltpu.make_async_copy(panel_hbm.at[band], panel_ref.at[band], sems.at[c]))
    small = [
        pltpu.make_async_copy(partner_hbm, partner_ref, sems.at[bands]),
    ]
    for copy in arriving + small:
        copy.start()
    order = {tile: n for n, tile in enumerate(tile_order(tiles))}
    rows, cols = grid_ids((TILE, TILE))
    metas = []

    def put(tile, value):
        value = value.astype(jnp.bfloat16)
        for row, owner, place, length in pieces(order[tile] * TILE, share):
            out_ref[owner, place : place + length, :] = value[row : row + length, :]

    for copy in arriving:
        copy.wait()
    for c in range(bands):
        low = 2 * c * TILE
        product = lax.dot_general(
            panel_ref[low:, :], panel_ref[low : low + 2 * TILE, :], NT, preferred_element_type=jnp.float32
        )
        for j in (2 * c, 2 * c + 1):
            for i in range(j + 1, tiles):
                put((i, j), product[i * TILE - low : (i + 1) * TILE - low, (j - 2 * c) * TILE : (j - 2 * c + 1) * TILE])
        first, second = product[:TILE, :TILE], product[TILE : 2 * TILE, TILE:]
        halved = jnp.where(rows == cols, 0.5 * second, second)
        put((2 * c, 2 * c), jnp.where(rows > cols, first, halved))
        metas.append((c, jnp.sum(jnp.where(rows == cols, 0.5 * first, 0.0), axis=0, keepdims=True)))

    owner_rows, _ = grid_ids((META, TILE))
    meta = jnp.zeros((META, TILE), jnp.float32)
    for n, diagonal in metas:
        meta = jnp.where(owner_rows == n, diagonal, meta)
    for copy in small:
        copy.wait()
    chrom = chrom_ref[0]
    for n, number in (
        (META_P0, lax.rem(partner_ref[0, 0], owners)),
        (META_P1, lax.rem(partner_ref[0, 1], owners)),
        (META_HI, chrom >> 4),
        (META_LO, chrom & 15),
    ):
        meta = jnp.where(owner_rows == n, number.astype(jnp.float32), meta)
    meta = meta.astype(jnp.bfloat16)
    for owner in range(owners):
        out_ref[owner, share : share + META, :] = meta


def mix_kernel(in_ref, out_ref):
    owners, height, _ = in_ref.shape
    share = height - META
    meta = in_ref[:, share:, :].astype(jnp.float32)

    def spread(n):
        return jnp.broadcast_to(meta[:, n : n + 1, :], (owners, SUB, TILE))

    def flat(value):
        return value.reshape(owners * SUB, TILE)

    high, low = spread(META_HI), spread(META_LO)
    same = jnp.where(
        (high[1:] == high[:-1]) & (low[1:] == low[:-1]), 1.0, 0.0
    )
    edge = jnp.zeros((1, SUB, TILE), jnp.float32)
    with_right = flat(jnp.concatenate([same, edge], axis=0))
    with_left = flat(jnp.concatenate([edge, same], axis=0))
    first, second = flat(spread(META_P0)), flat(spread(META_P1))
    rows, cols = grid_ids((owners * SUB, TILE))
    own = (rows // SUB).astype(jnp.float32)
    halves = []
    for h in range(owners * SUB // TILE):
        other = (cols // SUB + h * (TILE // SUB)).astype(jnp.float32)
        count = jnp.where(first == other, 1.0, 0.0) + jnp.where(second == other, 1.0, 0.0)
        count = count + jnp.where(own + 1.0 == other, with_right, 0.0) + jnp.where(own - 1.0 == other, with_left, 0.0)
        halves.append(jnp.where(rows % SUB == cols % SUB, count, 0.0))
    weights = jnp.concatenate(halves, axis=1).astype(jnp.bfloat16)

    groups = share // SUB
    for g in range(0, groups, 2):
        members = list(range(g, min(g + 2, groups)))
        stacked = jnp.concatenate(
            [in_ref[:, m * SUB : (m + 1) * SUB, :].reshape(owners * SUB, TILE) for m in members], axis=1
        )
        mixed = jnp.dot(weights, stacked, preferred_element_type=jnp.float32).astype(jnp.bfloat16)
        for n, m in enumerate(members):
            out_ref[:, m * SUB : (m + 1) * SUB, :] = mixed[:, n * TILE : (n + 1) * TILE].reshape(owners, SUB, TILE)
    padded = jnp.concatenate([meta, jnp.zeros((owners, SUB - META, TILE), jnp.float32)], axis=1)
    mixed = jnp.dot(
        weights, padded.reshape(owners * SUB, TILE).astype(jnp.bfloat16), preferred_element_type=jnp.float32
    )
    out_ref[:, share:, :] = mixed.reshape(owners, SUB, TILE)[:, :META, :].astype(jnp.bfloat16)


def finish_kernel(share, sums_ref, panel_ref, z_ref, out_ref, total_ref, half, scaled, first_iterate):
    samples, width = panel_ref.shape
    tiles = samples // TILE
    order = {tile: n for n, tile in enumerate(tile_order(tiles))}
    rows, cols = grid_ids((TILE, TILE))
    zero = jnp.zeros((TILE, TILE), jnp.bfloat16)

    def get(tile):
        return jnp.concatenate(
            [
                sums_ref[owner, place : place + length, :]
                for _, owner, place, length in pieces(order[tile] * TILE, share)
            ],
            axis=0,
        )

    def place(i, j, value):
        half[i * TILE : (i + 1) * TILE, j * TILE : (j + 1) * TILE] = value

    meta = sums_ref[0, share : share + META, :].astype(jnp.float32)
    for c in range(tiles // 2):
        for j in (2 * c, 2 * c + 1):
            for i in range(j + 1, tiles):
                place(i, j, get((i, j)))
        packed = get((2 * c, 2 * c)).astype(jnp.float32)
        lower = jnp.where(rows > cols, packed, jnp.where(rows == cols, meta[c : c + 1, :], 0.0))
        place(2 * c, 2 * c, lower.astype(jnp.bfloat16))
        place(2 * c + 1, 2 * c + 1, jnp.where(rows <= cols, packed, 0.0).astype(jnp.bfloat16))
        place(2 * c, 2 * c + 1, zero)

    parts = []
    for c in range(tiles // 2):
        low, top = 2 * c * TILE, (2 * c + 2) * TILE
        parts.append(
            jnp.dot(half[low:top, :top], panel_ref[:top, :], preferred_element_type=jnp.float32)
            * (leak_weight / samples)
            + 0.5 * panel_ref[low:top, :].astype(jnp.float32)
        )
    weighted = jnp.concatenate(parts, axis=0).astype(jnp.bfloat16)
    product = lax.dot_general(
        panel_ref[...], weighted, (((0,), (0,)), ((), ())), preferred_element_type=jnp.float32
    )
    wide_rows, wide_cols = grid_ids((width, width))
    matrix = product + product.T + jnp.where(wide_rows == wide_cols, ridge_term * samples, 0.0)
    norm = jnp.sqrt(jnp.sum(matrix * matrix, keepdims=True) + 1e-06 * samples * samples)
    matrix = matrix * (1.0 / norm)
    scaled[...] = matrix
    first_iterate[...] = jnp.where(wide_rows == wide_cols, 1.5, 0.0) - 0.5 * matrix

    eye = rows == cols
    blocks = width // TILE

    def to_column(ref, row):
        return jnp.sum(ref[...] * row, axis=1, keepdims=True)

    def to_row(ref, column):
        return jnp.sum(ref[...] * column, axis=0, keepdims=True)

    def turned_column(column):
        return jnp.concatenate(
            [
                jnp.sum(jnp.where(eye, column[n * TILE : (n + 1) * TILE], 0.0), axis=0, keepdims=True)
                for n in range(blocks)
            ],
            axis=1,
        )

    def turned_row(row):
        return jnp.concatenate(
            [
                jnp.sum(jnp.where(eye, row[:, n * TILE : (n + 1) * TILE], 0.0), axis=1, keepdims=True)
                for n in range(blocks)
            ],
            axis=0,
        )

    def second_iterate(column):
        inner = to_row(scaled, column)
        inner = to_column(first_iterate, inner)
        inner = to_row(first_iterate, inner)
        return 0.5 * to_column(first_iterate, 3.0 * turned_column(column) - inner)

    z_row = z_ref[...]
    product = second_iterate(second_iterate(to_column(scaled, z_row)))
    answer = 0.5 * second_iterate(3.0 * turned_row(z_row) - product)
    answer = turned_column(answer)
    out_ref[...] = answer
    total_ref[...] = jnp.broadcast_to(jnp.sum(answer * answer, keepdims=True).reshape(1, 1, 1), total_ref.shape)


def close_kernel(chroms, whitened_ref, group_ref, all_ref, out_ref, enrichment_ref):
    out_ref[...] = whitened_ref[...]
    overall = jnp.sum(all_ref[...], axis=0)
    enrichment_ref[...] = group_ref[0] * chroms / overall


def local(panel, zscores, block_chrom, lr_partner):
    samples, width = panel.shape
    owners = lax.axis_size("genome")
    chroms = lax.axis_size("chrom")
    tiles = samples // TILE
    share = len(tile_order(tiles)) * TILE // owners
    packed_shape = jax.ShapeDtypeStruct((owners, share + META, TILE), jnp.bfloat16)
    params = pltpu.CompilerParams(vmem_limit_bytes=48 * 2**20)

    lr_hbm, panel_hbm = (pltpu.with_memory_space_constraint(x, pltpu.HBM) for x in (lr_partner, panel))
    packed = pl.pallas_call(
        functools.partial(gram_kernel, owners, share),
        out_shape=packed_shape,
        in_specs=[HBM, SMEM, HBM],
        out_specs=VMEM,
        scratch_shapes=[
            pltpu.VMEM(panel.shape, panel.dtype),
            pltpu.SMEM(lr_partner.shape, jnp.int32),
            pltpu.SemaphoreType.DMA((tiles // 2 + 1,)),
        ],
        compiler_params=params,
    )(lr_hbm, block_chrom, panel_hbm)
    held = lax.all_to_all(packed, "genome", 0, 0, tiled=True)

    mixed = pl.pallas_call(
        mix_kernel,
        out_shape=packed_shape,
        in_specs=[VMEM],
        out_specs=VMEM,
        compiler_params=params,
    )(held)
    sums = lax.all_to_all(mixed, "genome", 0, 0, tiled=True)

    whitened, totals = pl.pallas_call(
        functools.partial(finish_kernel, share),
        out_shape=(
            jax.ShapeDtypeStruct((1, width), jnp.float32),
            jax.ShapeDtypeStruct((owners, 1, TILE), jnp.float32),
        ),
        in_specs=[VMEM] * 3,
        out_specs=(VMEM, VMEM),
        scratch_shapes=[
            pltpu.VMEM((samples, samples), jnp.bfloat16),
            pltpu.VMEM((width, width), jnp.float32),
            pltpu.VMEM((width, width), jnp.float32),
        ],
        compiler_params=params,
    )(sums, panel, zscores.reshape(1, width))

    of_group = lax.all_to_all(totals, "genome", 0, 0, tiled=True)
    group_sum = jnp.sum(of_group, axis=0, keepdims=True)
    of_all = lax.all_to_all(
        jnp.broadcast_to(group_sum, (chroms, 1, TILE)), "chrom", 0, 0, tiled=True
    )
    whitened, enrichment = pl.pallas_call(
        functools.partial(close_kernel, chroms),
        out_shape=(
            jax.ShapeDtypeStruct((1, width), jnp.float32),
            jax.ShapeDtypeStruct((1, TILE), jnp.float32),
        ),
        in_specs=[VMEM] * 3,
        out_specs=(VMEM, VMEM),
        compiler_params=params,
    )(whitened, group_sum, of_all)
    return (whitened.reshape(width), enrichment.reshape(TILE)[:1])


def solution(mesh):
    placed = (
        P(None, ("chrom", "genome")),
        P(("chrom", "genome")),
        P(("chrom", "genome")),
        P(("chrom", "genome"), None),
    )
    return jax.shard_map(
        local,
        mesh=mesh,
        in_specs=placed,
        out_specs=(P(("chrom", "genome")), P("chrom")),
        check_vma=False,
    )
```

```python
import functools

import jax
import jax.numpy as jnp
from jax import lax
from jax.experimental import pallas as pl
from jax.experimental.pallas import tpu as pltpu
from jax.sharding import PartitionSpec as P

ridge_term = 0.5
leak_weight = 0.25

TILE = 128
SUB = 16
META = 8
META_P0, META_P1, META_HI, META_LO = 3, 4, 5, 6

NT = (((1,), (1,)), ((), ()))
VMEM = pl.BlockSpec(memory_space=pltpu.VMEM)
HBM = pl.BlockSpec(memory_space=pltpu.HBM)
SMEM = pl.BlockSpec(memory_space=pltpu.SMEM)


def tile_order(tiles):
    below = [(i, j) for j in range(tiles) for i in range(j + 1, tiles)]
    return below + [(2 * c, 2 * c) for c in range(tiles // 2)]


def grid_ids(shape):
    return lax.broadcasted_iota(jnp.int32, shape, 0), lax.broadcasted_iota(jnp.int32, shape, 1)


def pieces(start, share):
    out, row = [], 0
    while row < TILE:
        owner, place = divmod(start + row, share)
        length = min(TILE - row, share - place)
        out.append((row, owner, place, length))
        row += length
    return out


def gram_kernel(owners, share, partner_hbm, chrom_ref, panel_hbm, out_ref, panel_ref, partner_ref, sems):
    samples = panel_ref.shape[0]
    tiles = samples // TILE
    bands = tiles // 2
    arriving = []
    for c in range(bands):
        band = pl.ds(2 * c * TILE, 2 * TILE)
        arriving.append(pltpu.make_async_copy(panel_hbm.at[band], panel_ref.at[band], sems.at[c]))
    small = [
        pltpu.make_async_copy(partner_hbm, partner_ref, sems.at[bands]),
    ]
    for copy in arriving + small:
        copy.start()
    order = {tile: n for n, tile in enumerate(tile_order(tiles))}
    rows, cols = grid_ids((TILE, TILE))
    metas = []

    def put(tile, value):
        value = value.astype(jnp.bfloat16)
        for row, owner, place, length in pieces(order[tile] * TILE, share):
            out_ref[owner, place : place + length, :] = value[row : row + length, :]

    for copy in arriving:
        copy.wait()
    for c in range(bands):
        low = 2 * c * TILE
        product = lax.dot_general(
            panel_ref[low:, :], panel_ref[low : low + 2 * TILE, :], NT, preferred_element_type=jnp.float32
        )
        for j in (2 * c, 2 * c + 1):
            for i in range(j + 1, tiles):
                put((i, j), product[i * TILE - low : (i + 1) * TILE - low, (j - 2 * c) * TILE : (j - 2 * c + 1) * TILE])
        first, second = product[:TILE, :TILE], product[TILE : 2 * TILE, TILE:]
        halved = jnp.where(rows == cols, 0.5 * second, second)
        put((2 * c, 2 * c), jnp.where(rows > cols, first, halved))
        metas.append((c, jnp.sum(jnp.where(rows == cols, 0.5 * first, 0.0), axis=0, keepdims=True)))

    owner_rows, _ = grid_ids((META, TILE))
    meta = jnp.zeros((META, TILE), jnp.float32)
    for n, diagonal in metas:
        meta = jnp.where(owner_rows == n, diagonal, meta)
    for copy in small:
        copy.wait()
    chrom = chrom_ref[0]
    for n, number in (
        (META_P0, lax.rem(partner_ref[0, 0], owners)),
        (META_P1, lax.rem(partner_ref[0, 1], owners)),
        (META_HI, chrom >> 4),
        (META_LO, chrom & 15),
    ):
        meta = jnp.where(owner_rows == n, number.astype(jnp.float32), meta)
    meta = meta.astype(jnp.bfloat16)
    for owner in range(owners):
        out_ref[owner, share : share + META, :] = meta


def mix_kernel(in_ref, out_ref):
    owners, height, _ = in_ref.shape
    share = height - META
    meta = in_ref[:, share:, :].astype(jnp.float32)

    def spread(n):
        return jnp.broadcast_to(meta[:, n : n + 1, :], (owners, SUB, TILE))

    def flat(value):
        return value.reshape(owners * SUB, TILE)

    high, low = spread(META_HI), spread(META_LO)
    same = jnp.where(
        (high[1:] == high[:-1]) & (low[1:] == low[:-1]), 1.0, 0.0
    )
    edge = jnp.zeros((1, SUB, TILE), jnp.float32)
    with_right = flat(jnp.concatenate([same, edge], axis=0))
    with_left = flat(jnp.concatenate([edge, same], axis=0))
    first, second = flat(spread(META_P0)), flat(spread(META_P1))
    rows, cols = grid_ids((owners * SUB, TILE))
    own = (rows // SUB).astype(jnp.float32)
    halves = []
    for h in range(owners * SUB // TILE):
        other = (cols // SUB + h * (TILE // SUB)).astype(jnp.float32)
        count = jnp.where(first == other, 1.0, 0.0) + jnp.where(second == other, 1.0, 0.0)
        count = count + jnp.where(own + 1.0 == other, with_right, 0.0) + jnp.where(own - 1.0 == other, with_left, 0.0)
        halves.append(jnp.where(rows % SUB == cols % SUB, count, 0.0))
    weights = jnp.concatenate(halves, axis=1).astype(jnp.bfloat16)

    groups = share // SUB
    for g in range(0, groups, 2):
        members = list(range(g, min(g + 2, groups)))
        stacked = jnp.concatenate(
            [in_ref[:, m * SUB : (m + 1) * SUB, :].reshape(owners * SUB, TILE) for m in members], axis=1
        )
        mixed = jnp.dot(weights, stacked, preferred_element_type=jnp.float32).astype(jnp.bfloat16)
        for n, m in enumerate(members):
            out_ref[:, m * SUB : (m + 1) * SUB, :] = mixed[:, n * TILE : (n + 1) * TILE].reshape(owners, SUB, TILE)
    padded = jnp.concatenate([meta, jnp.zeros((owners, SUB - META, TILE), jnp.float32)], axis=1)
    mixed = jnp.dot(
        weights, padded.reshape(owners * SUB, TILE).astype(jnp.bfloat16), preferred_element_type=jnp.float32
    )
    out_ref[:, share:, :] = mixed.reshape(owners, SUB, TILE)[:, :META, :].astype(jnp.bfloat16)


def finish_kernel(share, sums_ref, panel_ref, z_ref, out_ref, total_ref, half, whole, shifted):
    samples, width = panel_ref.shape
    tiles = samples // TILE
    order = {tile: n for n, tile in enumerate(tile_order(tiles))}
    rows, cols = grid_ids((TILE, TILE))
    zero = jnp.zeros((TILE, TILE), jnp.bfloat16)

    def get(tile):
        return jnp.concatenate(
            [
                sums_ref[owner, place : place + length, :]
                for _, owner, place, length in pieces(order[tile] * TILE, share)
            ],
            axis=0,
        )

    def place(i, j, value):
        half[i * TILE : (i + 1) * TILE, j * TILE : (j + 1) * TILE] = value

    meta = sums_ref[0, share : share + META, :].astype(jnp.float32)
    for c in range(tiles // 2):
        for j in (2 * c, 2 * c + 1):
            for i in range(j + 1, tiles):
                place(i, j, get((i, j)))
        packed = get((2 * c, 2 * c)).astype(jnp.float32)
        lower = jnp.where(rows > cols, packed, jnp.where(rows == cols, meta[c : c + 1, :], 0.0))
        place(2 * c, 2 * c, lower.astype(jnp.bfloat16))
        place(2 * c + 1, 2 * c + 1, jnp.where(rows <= cols, packed, 0.0).astype(jnp.bfloat16))
        place(2 * c, 2 * c + 1, zero)

    parts = []
    for c in range(tiles // 2):
        low, top = 2 * c * TILE, (2 * c + 2) * TILE
        parts.append(
            jnp.dot(half[low:top, :top], panel_ref[:top, :], preferred_element_type=jnp.float32)
            * (leak_weight / samples)
            + 0.5 * panel_ref[low:top, :].astype(jnp.float32)
        )
    weighted = jnp.concatenate(parts, axis=0).astype(jnp.bfloat16)
    product = lax.dot_general(
        panel_ref[...], weighted, (((0,), (0,)), ((), ())), preferred_element_type=jnp.float32
    )
    wide = width // TILE
    eye = rows == cols
    ridge = jnp.where(eye, ridge_term * samples, 0.0)
    both = product + product.T

    def with_ridge(m):
        own, above = m * TILE, (m + 1) * TILE
        band = both[own:above]
        return jnp.concatenate([band[:, :own], band[:, own:above] + ridge, band[:, above:]][(m == 0):(2 if m == wide - 1 else 3)], axis=1)

    matrix = jnp.concatenate([with_ridge(m) for m in range(wide)], axis=0)
    whole[...] = matrix
    shifted[...] = matrix
    norm = jnp.sqrt(jnp.sum(matrix * matrix, keepdims=True) + 1e-06 * samples * samples)
    inverse = 1.0 / norm
    for n in range(wide):
        own = slice(n * TILE, (n + 1) * TILE)
        shifted[own, own] = whole[own, own] - jnp.where(eye, 3.0 * norm, 0.0)

    def to_column(ref, row):
        return jnp.sum(ref[...] * row, axis=1, keepdims=True)

    def to_row(ref, column):
        return jnp.sum(ref[...] * column, axis=0, keepdims=True)

    def turned_column(column):
        return jnp.concatenate(
            [
                jnp.sum(jnp.where(eye, column[n * TILE : (n + 1) * TILE], 0.0), axis=0, keepdims=True)
                for n in range(wide)
            ],
            axis=1,
        )

    def turned_row(row):
        return jnp.concatenate(
            [
                jnp.sum(jnp.where(eye, row[:, n * TILE : (n + 1) * TILE], 0.0), axis=1, keepdims=True)
                for n in range(wide)
            ],
            axis=0,
        )

    def second_iterate(column, factor):
        inner = to_row(whole, column) * inverse
        inner = to_row(shifted, to_column(shifted, inner)) * (0.25 * inverse * inverse)
        return to_column(shifted, (3.0 * turned_column(column) - inner) * ((-0.25 * factor) * inverse))

    z_row = z_ref[...]
    product = second_iterate(second_iterate(to_column(whole, z_row * inverse), 1.0), 1.0)
    answer = second_iterate(3.0 * turned_row(z_row) - product, 0.5)
    answer = turned_column(answer)
    out_ref[...] = answer
    total_ref[...] = jnp.broadcast_to(jnp.sum(answer * answer, keepdims=True).reshape(1, 1, 1), total_ref.shape)


def close_kernel(chroms, whitened_ref, group_ref, all_ref, out_ref, enrichment_ref):
    out_ref[...] = whitened_ref[...]
    overall = jnp.sum(all_ref[...], axis=0)
    enrichment_ref[...] = group_ref[0] * chroms / overall


def local(panel, zscores, block_chrom, lr_partner):
    samples, width = panel.shape
    owners = lax.axis_size("genome")
    chroms = lax.axis_size("chrom")
    tiles = samples // TILE
    share = len(tile_order(tiles)) * TILE // owners
    packed_shape = jax.ShapeDtypeStruct((owners, share + META, TILE), jnp.bfloat16)
    params = pltpu.CompilerParams(vmem_limit_bytes=48 * 2**20)

    lr_hbm, panel_hbm = (pltpu.with_memory_space_constraint(x, pltpu.HBM) for x in (lr_partner, panel))
    packed = pl.pallas_call(
        functools.partial(gram_kernel, owners, share),
        out_shape=packed_shape,
        in_specs=[HBM, SMEM, HBM],
        out_specs=VMEM,
        scratch_shapes=[
            pltpu.VMEM(panel.shape, panel.dtype),
            pltpu.SMEM(lr_partner.shape, jnp.int32),
            pltpu.SemaphoreType.DMA((tiles // 2 + 1,)),
        ],
        compiler_params=params,
    )(lr_hbm, block_chrom, panel_hbm)
    held = lax.all_to_all(packed, "genome", 0, 0, tiled=True)

    mixed = pl.pallas_call(
        mix_kernel,
        out_shape=packed_shape,
        in_specs=[VMEM],
        out_specs=VMEM,
        compiler_params=params,
    )(held)
    sums = lax.all_to_all(mixed, "genome", 0, 0, tiled=True)

    whitened, totals = pl.pallas_call(
        functools.partial(finish_kernel, share),
        out_shape=(
            jax.ShapeDtypeStruct((1, width), jnp.float32),
            jax.ShapeDtypeStruct((owners, 1, TILE), jnp.float32),
        ),
        in_specs=[VMEM] * 3,
        out_specs=(VMEM, VMEM),
        scratch_shapes=[
            pltpu.VMEM((samples, samples), jnp.bfloat16),
            pltpu.VMEM((width, width), jnp.float32),
            pltpu.VMEM((width, width), jnp.float32),
        ],
        compiler_params=params,
    )(sums, panel, zscores.reshape(1, width))

    of_group = lax.all_to_all(totals, "genome", 0, 0, tiled=True)
    group_sum = jnp.sum(of_group, axis=0, keepdims=True)
    of_all = lax.all_to_all(
        jnp.broadcast_to(group_sum, (chroms, 1, TILE)), "chrom", 0, 0, tiled=True
    )
    whitened, enrichment = pl.pallas_call(
        functools.partial(close_kernel, chroms),
        out_shape=(
            jax.ShapeDtypeStruct((1, width), jnp.float32),
            jax.ShapeDtypeStruct((1, TILE), jnp.float32),
        ),
        in_specs=[VMEM] * 3,
        out_specs=(VMEM, VMEM),
        compiler_params=params,
    )(whitened, group_sum, of_all)
    return (whitened.reshape(width), enrichment.reshape(TILE)[:1])


def solution(mesh):
    placed = (
        P(None, ("chrom", "genome")),
        P(("chrom", "genome")),
        P(("chrom", "genome")),
        P(("chrom", "genome"), None),
    )
    return jax.shard_map(
        local,
        mesh=mesh,
        in_specs=placed,
        out_specs=(P(("chrom", "genome")), P("chrom")),
        check_vma=False,
    )
```

```python
import functools

import jax
import jax.numpy as jnp
from jax import lax
from jax.experimental import pallas as pl
from jax.experimental.pallas import tpu as pltpu
from jax.sharding import PartitionSpec as P

ridge_term = 0.5
leak_weight = 0.25

TILE = 128
SUB = 16
META = 8
META_P0, META_P1, META_HI, META_LO = 3, 4, 5, 6

NT = (((1,), (1,)), ((), ()))
VMEM = pl.BlockSpec(memory_space=pltpu.VMEM)
HBM = pl.BlockSpec(memory_space=pltpu.HBM)
SMEM = pl.BlockSpec(memory_space=pltpu.SMEM)


def tile_order(tiles):
    below = [(i, j) for j in range(tiles) for i in range(j + 1, tiles)]
    return below + [(2 * c, 2 * c) for c in range(tiles // 2)]


def grid_ids(shape):
    return lax.broadcasted_iota(jnp.int32, shape, 0), lax.broadcasted_iota(jnp.int32, shape, 1)


def pieces(start, share):
    out, row = [], 0
    while row < TILE:
        owner, place = divmod(start + row, share)
        length = min(TILE - row, share - place)
        out.append((row, owner, place, length))
        row += length
    return out


def gram_kernel(owners, share, partner_hbm, chrom_ref, panel_hbm, out_ref, panel_ref, partner_ref, sems):
    samples = panel_ref.shape[0]
    tiles = samples // TILE
    bands = tiles // 2
    arriving = []
    for c in range(bands):
        band = pl.ds(2 * c * TILE, 2 * TILE)
        arriving.append(pltpu.make_async_copy(panel_hbm.at[band], panel_ref.at[band], sems.at[c]))
    small = [
        pltpu.make_async_copy(partner_hbm, partner_ref, sems.at[bands]),
    ]
    for copy in arriving + small:
        copy.start()
    order = {tile: n for n, tile in enumerate(tile_order(tiles))}
    rows, cols = grid_ids((TILE, TILE))
    metas = []

    def put(tile, value):
        value = value.astype(jnp.bfloat16)
        for row, owner, place, length in pieces(order[tile] * TILE, share):
            out_ref[owner, place : place + length, :] = value[row : row + length, :]

    for copy in arriving:
        copy.wait()
    for c in range(bands):
        low = 2 * c * TILE
        product = lax.dot_general(
            panel_ref[low:, :], panel_ref[low : low + 2 * TILE, :], NT, preferred_element_type=jnp.float32
        )
        for j in (2 * c, 2 * c + 1):
            for i in range(j + 1, tiles):
                put((i, j), product[i * TILE - low : (i + 1) * TILE - low, (j - 2 * c) * TILE : (j - 2 * c + 1) * TILE])
        first, second = product[:TILE, :TILE], product[TILE : 2 * TILE, TILE:]
        halved = jnp.where(rows == cols, 0.5 * second, second)
        put((2 * c, 2 * c), jnp.where(rows > cols, first, halved))
        metas.append((c, jnp.sum(jnp.where(rows == cols, 0.5 * first, 0.0), axis=0, keepdims=True)))

    owner_rows, _ = grid_ids((META, TILE))
    meta = jnp.zeros((META, TILE), jnp.float32)
    for n, diagonal in metas:
        meta = jnp.where(owner_rows == n, diagonal, meta)
    for copy in small:
        copy.wait()
    chrom = chrom_ref[0]
    for n, number in (
        (META_P0, lax.rem(partner_ref[0, 0], owners)),
        (META_P1, lax.rem(partner_ref[0, 1], owners)),
        (META_HI, chrom >> 4),
        (META_LO, chrom & 15),
    ):
        meta = jnp.where(owner_rows == n, number.astype(jnp.float32), meta)
    meta = meta.astype(jnp.bfloat16)
    for owner in range(owners):
        out_ref[owner, share : share + META, :] = meta


def mix_kernel(in_ref, out_ref, diagonal_ref):
    owners, height, _ = in_ref.shape
    share = height - META
    meta = in_ref[:, share:, :].astype(jnp.float32)

    def spread(n):
        return jnp.broadcast_to(meta[:, n : n + 1, :], (owners, SUB, TILE))

    def flat(value):
        return value.reshape(owners * SUB, TILE)

    high, low = spread(META_HI), spread(META_LO)
    same = jnp.where(
        (high[1:] == high[:-1]) & (low[1:] == low[:-1]), 1.0, 0.0
    )
    edge = jnp.zeros((1, SUB, TILE), jnp.float32)
    with_right = flat(jnp.concatenate([same, edge], axis=0))
    with_left = flat(jnp.concatenate([edge, same], axis=0))
    first, second = flat(spread(META_P0)), flat(spread(META_P1))
    rows, cols = grid_ids((owners * SUB, TILE))
    own = (rows // SUB).astype(jnp.float32)
    halves = []
    for h in range(owners * SUB // TILE):
        other = (cols // SUB + h * (TILE // SUB)).astype(jnp.float32)
        count = jnp.where(first == other, 1.0, 0.0) + jnp.where(second == other, 1.0, 0.0)
        count = count + jnp.where(own + 1.0 == other, with_right, 0.0) + jnp.where(own - 1.0 == other, with_left, 0.0)
        halves.append(jnp.where(rows % SUB == cols % SUB, count, 0.0))
    weights = jnp.concatenate(halves, axis=1).astype(jnp.bfloat16)

    groups = share // SUB
    for g in range(0, groups, 2):
        members = list(range(g, min(g + 2, groups)))
        stacked = jnp.concatenate(
            [in_ref[:, m * SUB : (m + 1) * SUB, :].reshape(owners * SUB, TILE) for m in members], axis=1
        )
        mixed = jnp.dot(weights, stacked, preferred_element_type=jnp.float32).astype(jnp.bfloat16)
        for n, m in enumerate(members):
            out_ref[:, m * SUB : (m + 1) * SUB, :] = mixed[:, n * TILE : (n + 1) * TILE].reshape(owners, SUB, TILE)
    padded = jnp.concatenate([meta, jnp.zeros((owners, SUB - META, TILE), jnp.float32)], axis=1)
    mixed = jnp.dot(
        weights, padded.reshape(owners * SUB, TILE).astype(jnp.bfloat16), preferred_element_type=jnp.float32
    )
    diagonal_ref[...] = mixed.reshape(owners, SUB, TILE)[:, :META, :]


def finish_kernel(share, sums_ref, diagonal_ref, panel_ref, z_hbm, out_ref, total_ref, half, whole, shifted, z_ref, sem):
    arriving = pltpu.make_async_copy(z_hbm, z_ref, sem)
    arriving.start()
    samples, width = panel_ref.shape
    tiles = samples // TILE
    order = {tile: n for n, tile in enumerate(tile_order(tiles))}
    rows, cols = grid_ids((TILE, TILE))
    zero = jnp.zeros((TILE, TILE), jnp.bfloat16)

    def get(tile):
        return jnp.concatenate(
            [
                sums_ref[owner, place : place + length, :]
                for _, owner, place, length in pieces(order[tile] * TILE, share)
            ],
            axis=0,
        )

    def place(i, j, value):
        half[i * TILE : (i + 1) * TILE, j * TILE : (j + 1) * TILE] = value

    meta = diagonal_ref[lax.axis_index("genome")]
    for c in range(tiles // 2):
        for j in (2 * c, 2 * c + 1):
            for i in range(j + 1, tiles):
                place(i, j, get((i, j)))
        packed = get((2 * c, 2 * c)).astype(jnp.float32)
        lower = jnp.where(rows > cols, packed, jnp.where(rows == cols, meta[c : c + 1, :], 0.0))
        place(2 * c, 2 * c, lower.astype(jnp.bfloat16))
        place(2 * c + 1, 2 * c + 1, jnp.where(rows <= cols, packed, 0.0).astype(jnp.bfloat16))
        place(2 * c, 2 * c + 1, zero)

    parts = []
    for c in range(tiles // 2):
        low, top = 2 * c * TILE, (2 * c + 2) * TILE
        parts.append(
            jnp.dot(half[low:top, :top], panel_ref[:top, :], preferred_element_type=jnp.float32)
            * (leak_weight / samples)
            + 0.5 * panel_ref[low:top, :].astype(jnp.float32)
        )
    weighted = jnp.concatenate(parts, axis=0).astype(jnp.bfloat16)
    product = lax.dot_general(
        panel_ref[...], weighted, (((0,), (0,)), ((), ())), preferred_element_type=jnp.float32
    )
    wide = width // TILE
    eye = rows == cols
    ridge = jnp.where(eye, ridge_term * samples, 0.0)
    both = product + product.T

    def with_ridge(m):
        own, above = m * TILE, (m + 1) * TILE
        band = both[own:above]
        return jnp.concatenate([band[:, :own], band[:, own:above] + ridge, band[:, above:]][(m == 0):(2 if m == wide - 1 else 3)], axis=1)

    matrix = jnp.concatenate([with_ridge(m) for m in range(wide)], axis=0)
    whole[...] = matrix
    shifted[...] = matrix
    norm = jnp.sqrt(jnp.sum(matrix * matrix, keepdims=True) + 1e-06 * samples * samples)
    inverse = 1.0 / norm
    for n in range(wide):
        own = slice(n * TILE, (n + 1) * TILE)
        shifted[own, own] = whole[own, own] - jnp.where(eye, 3.0 * norm, 0.0)

    def to_column(ref, row):
        return jnp.sum(ref[...] * row, axis=1, keepdims=True)

    def to_row(ref, column):
        return jnp.sum(ref[...] * column, axis=0, keepdims=True)

    def turned_column(column):
        return jnp.concatenate(
            [
                jnp.sum(jnp.where(eye, column[n * TILE : (n + 1) * TILE], 0.0), axis=0, keepdims=True)
                for n in range(wide)
            ],
            axis=1,
        )

    def turned_row(row):
        return jnp.concatenate(
            [
                jnp.sum(jnp.where(eye, row[:, n * TILE : (n + 1) * TILE], 0.0), axis=1, keepdims=True)
                for n in range(wide)
            ],
            axis=0,
        )

    def second_iterate(column, factor):
        inner = to_row(whole, column) * inverse
        inner = to_row(shifted, to_column(shifted, inner)) * (0.25 * inverse * inverse)
        return to_column(shifted, (3.0 * turned_column(column) - inner) * ((-0.25 * factor) * inverse))

    arriving.wait()
    z_row = z_ref[...]
    product = second_iterate(second_iterate(to_column(whole, z_row * inverse), 1.0), 1.0)
    answer = second_iterate(3.0 * turned_row(z_row) - product, 0.5)
    answer = turned_column(answer)
    out_ref[...] = answer
    total_ref[...] = jnp.broadcast_to(jnp.sum(answer * answer, keepdims=True).reshape(1, 1, 1), total_ref.shape)


def close_kernel(chroms, whitened_ref, group_ref, all_ref, out_ref, enrichment_ref):
    out_ref[...] = whitened_ref[...]
    overall = jnp.sum(all_ref[...], axis=0)
    enrichment_ref[...] = group_ref[0] * chroms / overall


def local(panel, zscores, block_chrom, lr_partner):
    samples, width = panel.shape
    owners = lax.axis_size("genome")
    chroms = lax.axis_size("chrom")
    tiles = samples // TILE
    share = len(tile_order(tiles)) * TILE // owners
    packed_shape = jax.ShapeDtypeStruct((owners, share + META, TILE), jnp.bfloat16)
    params = pltpu.CompilerParams(vmem_limit_bytes=48 * 2**20)

    lr_hbm, panel_hbm = (pltpu.with_memory_space_constraint(x, pltpu.HBM) for x in (lr_partner, panel))
    packed = pl.pallas_call(
        functools.partial(gram_kernel, owners, share),
        out_shape=packed_shape,
        in_specs=[HBM, SMEM, HBM],
        out_specs=VMEM,
        scratch_shapes=[
            pltpu.VMEM(panel.shape, panel.dtype),
            pltpu.SMEM(lr_partner.shape, jnp.int32),
            pltpu.SemaphoreType.DMA((tiles // 2 + 1,)),
        ],
        compiler_params=params,
    )(lr_hbm, block_chrom, panel_hbm)
    held = lax.all_to_all(packed, "genome", 0, 0, tiled=True)

    mixed, diagonals = pl.pallas_call(
        mix_kernel,
        out_shape=(
            jax.ShapeDtypeStruct((owners, share, TILE), jnp.bfloat16),
            jax.ShapeDtypeStruct((owners, META, TILE), jnp.float32),
        ),
        in_specs=[VMEM],
        out_specs=(VMEM, VMEM),
        compiler_params=params,
    )(held)
    sums = lax.all_to_all(mixed, "genome", 0, 0, tiled=True)

    whitened, totals = pl.pallas_call(
        functools.partial(finish_kernel, share),
        out_shape=(
            jax.ShapeDtypeStruct((1, width), jnp.float32),
            jax.ShapeDtypeStruct((owners, 1, TILE), jnp.float32),
        ),
        in_specs=[VMEM, VMEM, VMEM, HBM],
        out_specs=(VMEM, VMEM),
        scratch_shapes=[
            pltpu.VMEM((samples, samples), jnp.bfloat16),
            pltpu.VMEM((width, width), jnp.float32),
            pltpu.VMEM((width, width), jnp.float32),
            pltpu.VMEM((1, width), jnp.float32),
            pltpu.SemaphoreType.DMA,
        ],
        compiler_params=params,
    )(sums, diagonals, panel, pltpu.with_memory_space_constraint(zscores.reshape(1, width), pltpu.HBM))

    of_group = lax.all_to_all(totals, "genome", 0, 0, tiled=True)
    group_sum = jnp.sum(of_group, axis=0, keepdims=True)
    of_all = lax.all_to_all(
        jnp.broadcast_to(group_sum, (chroms, 1, TILE)), "chrom", 0, 0, tiled=True
    )
    whitened, enrichment = pl.pallas_call(
        functools.partial(close_kernel, chroms),
        out_shape=(
            jax.ShapeDtypeStruct((1, width), jnp.float32),
            jax.ShapeDtypeStruct((1, TILE), jnp.float32),
        ),
        in_specs=[VMEM] * 3,
        out_specs=(VMEM, VMEM),
        compiler_params=params,
    )(whitened, group_sum, of_all)
    return (whitened.reshape(width), enrichment.reshape(TILE)[:1])


def solution(mesh):
    placed = (
        P(None, ("chrom", "genome")),
        P(("chrom", "genome")),
        P(("chrom", "genome")),
        P(("chrom", "genome"), None),
    )
    return jax.shard_map(
        local,
        mesh=mesh,
        in_specs=placed,
        out_specs=(P(("chrom", "genome")), P("chrom")),
        check_vma=False,
    )
```

```python
import functools

import jax
import jax.numpy as jnp
from jax import lax
from jax.experimental import pallas as pl
from jax.experimental.pallas import tpu as pltpu
from jax.sharding import PartitionSpec as P

ridge_term = 0.5
leak_weight = 0.25

TILE = 128
SUB = 16
META = 8
META_P0, META_P1, META_HI, META_LO = 3, 4, 5, 6

NT = (((1,), (1,)), ((), ()))
VMEM = pl.BlockSpec(memory_space=pltpu.VMEM)
HBM = pl.BlockSpec(memory_space=pltpu.HBM)
SMEM = pl.BlockSpec(memory_space=pltpu.SMEM)


def tile_order(tiles):
    below = [(i, j) for j in range(tiles) for i in range(j + 1, tiles)]
    return below + [(2 * c, 2 * c) for c in range(tiles // 2)]


def grid_ids(shape):
    return lax.broadcasted_iota(jnp.int32, shape, 0), lax.broadcasted_iota(jnp.int32, shape, 1)


def pieces(start, share):
    out, row = [], 0
    while row < TILE:
        owner, place = divmod(start + row, share)
        length = min(TILE - row, share - place)
        out.append((row, owner, place, length))
        row += length
    return out


def gram_kernel(owners, share, partner_hbm, chrom_ref, panel_hbm, z_hbm, out_ref, z_ref, panel_ref, partner_ref, sems):
    samples = panel_ref.shape[0]
    tiles = samples // TILE
    bands = tiles // 2
    arriving = []
    for c in range(bands):
        band = pl.ds(2 * c * TILE, 2 * TILE)
        arriving.append(pltpu.make_async_copy(panel_hbm.at[band], panel_ref.at[band], sems.at[c]))
    small = [
        pltpu.make_async_copy(partner_hbm, partner_ref, sems.at[bands]),
        pltpu.make_async_copy(z_hbm, z_ref, sems.at[bands + 1]),
    ]
    for copy in arriving + small:
        copy.start()
    order = {tile: n for n, tile in enumerate(tile_order(tiles))}
    rows, cols = grid_ids((TILE, TILE))
    metas = []

    def put(tile, value):
        value = value.astype(jnp.bfloat16)
        for row, owner, place, length in pieces(order[tile] * TILE, share):
            out_ref[owner, place : place + length, :] = value[row : row + length, :]

    for copy in arriving:
        copy.wait()
    for c in range(bands):
        low = 2 * c * TILE
        product = lax.dot_general(
            panel_ref[low:, :], panel_ref[low : low + 2 * TILE, :], NT, preferred_element_type=jnp.float32
        )
        for j in (2 * c, 2 * c + 1):
            for i in range(j + 1, tiles):
                put((i, j), product[i * TILE - low : (i + 1) * TILE - low, (j - 2 * c) * TILE : (j - 2 * c + 1) * TILE])
        first, second = product[:TILE, :TILE], product[TILE : 2 * TILE, TILE:]
        halved = jnp.where(rows == cols, 0.5 * second, second)
        put((2 * c, 2 * c), jnp.where(rows > cols, first, halved))
        metas.append((c, jnp.sum(jnp.where(rows == cols, 0.5 * first, 0.0), axis=0, keepdims=True)))

    owner_rows, _ = grid_ids((META, TILE))
    meta = jnp.zeros((META, TILE), jnp.float32)
    for n, diagonal in metas:
        meta = jnp.where(owner_rows == n, diagonal, meta)
    for copy in small:
        copy.wait()
    chrom = chrom_ref[0]
    for n, number in (
        (META_P0, lax.rem(partner_ref[0, 0], owners)),
        (META_P1, lax.rem(partner_ref[0, 1], owners)),
        (META_HI, chrom >> 4),
        (META_LO, chrom & 15),
    ):
        meta = jnp.where(owner_rows == n, number.astype(jnp.float32), meta)
    meta = meta.astype(jnp.bfloat16)
    for owner in range(owners):
        out_ref[owner, share : share + META, :] = meta


def mix_kernel(in_ref, out_ref, diagonal_ref):
    owners, height, _ = in_ref.shape
    share = height - META
    meta = in_ref[:, share:, :].astype(jnp.float32)

    def spread(n):
        return jnp.broadcast_to(meta[:, n : n + 1, :], (owners, SUB, TILE))

    def flat(value):
        return value.reshape(owners * SUB, TILE)

    high, low = spread(META_HI), spread(META_LO)
    same = jnp.where(
        (high[1:] == high[:-1]) & (low[1:] == low[:-1]), 1.0, 0.0
    )
    edge = jnp.zeros((1, SUB, TILE), jnp.float32)
    with_right = flat(jnp.concatenate([same, edge], axis=0))
    with_left = flat(jnp.concatenate([edge, same], axis=0))
    first, second = flat(spread(META_P0)), flat(spread(META_P1))
    rows, cols = grid_ids((owners * SUB, TILE))
    own = (rows // SUB).astype(jnp.float32)
    halves = []
    for h in range(owners * SUB // TILE):
        other = (cols // SUB + h * (TILE // SUB)).astype(jnp.float32)
        count = jnp.where(first == other, 1.0, 0.0) + jnp.where(second == other, 1.0, 0.0)
        count = count + jnp.where(own + 1.0 == other, with_right, 0.0) + jnp.where(own - 1.0 == other, with_left, 0.0)
        halves.append(jnp.where(rows % SUB == cols % SUB, count, 0.0))
    weights = jnp.concatenate(halves, axis=1).astype(jnp.bfloat16)

    groups = share // SUB
    for g in range(0, groups, 2):
        members = list(range(g, min(g + 2, groups)))
        stacked = jnp.concatenate(
            [in_ref[:, m * SUB : (m + 1) * SUB, :].reshape(owners * SUB, TILE) for m in members], axis=1
        )
        mixed = jnp.dot(weights, stacked, preferred_element_type=jnp.float32).astype(jnp.bfloat16)
        for n, m in enumerate(members):
            out_ref[:, m * SUB : (m + 1) * SUB, :] = mixed[:, n * TILE : (n + 1) * TILE].reshape(owners, SUB, TILE)
    padded = jnp.concatenate([meta, jnp.zeros((owners, SUB - META, TILE), jnp.float32)], axis=1)
    mixed = jnp.dot(
        weights, padded.reshape(owners * SUB, TILE).astype(jnp.bfloat16), preferred_element_type=jnp.float32
    )
    diagonal_ref[...] = mixed.reshape(owners, SUB, TILE)[:, :META, :]


def finish_kernel(share, sums_ref, diagonal_ref, panel_ref, z_ref, out_ref, total_ref, half, whole, shifted):
    samples, width = panel_ref.shape
    tiles = samples // TILE
    order = {tile: n for n, tile in enumerate(tile_order(tiles))}
    rows, cols = grid_ids((TILE, TILE))
    zero = jnp.zeros((TILE, TILE), jnp.bfloat16)

    def get(tile):
        return jnp.concatenate(
            [
                sums_ref[owner, place : place + length, :]
                for _, owner, place, length in pieces(order[tile] * TILE, share)
            ],
            axis=0,
        )

    def place(i, j, value):
        half[i * TILE : (i + 1) * TILE, j * TILE : (j + 1) * TILE] = value

    meta = diagonal_ref[lax.axis_index("genome")]
    for c in range(tiles // 2):
        for j in (2 * c, 2 * c + 1):
            for i in range(j + 1, tiles):
                place(i, j, get((i, j)))
        packed = get((2 * c, 2 * c)).astype(jnp.float32)
        lower = jnp.where(rows > cols, packed, jnp.where(rows == cols, meta[c : c + 1, :], 0.0))
        place(2 * c, 2 * c, lower.astype(jnp.bfloat16))
        place(2 * c + 1, 2 * c + 1, jnp.where(rows <= cols, packed, 0.0).astype(jnp.bfloat16))
        place(2 * c, 2 * c + 1, zero)

    parts = []
    for c in range(tiles // 2):
        low, top = 2 * c * TILE, (2 * c + 2) * TILE
        parts.append(
            jnp.dot(half[low:top, :top], panel_ref[:top, :], preferred_element_type=jnp.float32)
            * (leak_weight / samples)
            + 0.5 * panel_ref[low:top, :].astype(jnp.float32)
        )
    weighted = jnp.concatenate(parts, axis=0).astype(jnp.bfloat16)
    product = lax.dot_general(
        panel_ref[...], weighted, (((0,), (0,)), ((), ())), preferred_element_type=jnp.float32
    )
    wide = width // TILE
    eye = rows == cols
    ridge = jnp.where(eye, ridge_term * samples, 0.0)
    both = product + product.T

    def with_ridge(m):
        own, above = m * TILE, (m + 1) * TILE
        band = both[own:above]
        return jnp.concatenate([band[:, :own], band[:, own:above] + ridge, band[:, above:]][(m == 0):(2 if m == wide - 1 else 3)], axis=1)

    matrix = jnp.concatenate([with_ridge(m) for m in range(wide)], axis=0)
    whole[...] = matrix
    shifted[...] = matrix
    norm = jnp.sqrt(jnp.sum(matrix * matrix, keepdims=True) + 1e-06 * samples * samples)
    inverse = 1.0 / norm
    for n in range(wide):
        own = slice(n * TILE, (n + 1) * TILE)
        shifted[own, own] = whole[own, own] - jnp.where(eye, 3.0 * norm, 0.0)

    def to_column(ref, row):
        return jnp.sum(ref[...] * row, axis=1, keepdims=True)

    def to_row(ref, column):
        return jnp.sum(ref[...] * column, axis=0, keepdims=True)

    def turned_column(column):
        return jnp.concatenate(
            [
                jnp.sum(jnp.where(eye, column[n * TILE : (n + 1) * TILE], 0.0), axis=0, keepdims=True)
                for n in range(wide)
            ],
            axis=1,
        )

    def turned_row(row):
        return jnp.concatenate(
            [
                jnp.sum(jnp.where(eye, row[:, n * TILE : (n + 1) * TILE], 0.0), axis=1, keepdims=True)
                for n in range(wide)
            ],
            axis=0,
        )

    def second_iterate(column, factor):
        inner = to_row(whole, column) * inverse
        inner = to_row(shifted, to_column(shifted, inner)) * (0.25 * inverse * inverse)
        return to_column(shifted, (3.0 * turned_column(column) - inner) * ((-0.25 * factor) * inverse))

    z_row = z_ref[...]
    product = second_iterate(second_iterate(to_column(whole, z_row * inverse), 1.0), 1.0)
    answer = second_iterate(3.0 * turned_row(z_row) - product, 0.5)
    answer = turned_column(answer)
    out_ref[...] = answer
    total_ref[...] = jnp.broadcast_to(jnp.sum(answer * answer, keepdims=True).reshape(1, 1, 1), total_ref.shape)


def close_kernel(chroms, whitened_ref, group_ref, all_ref, out_ref, enrichment_ref):
    out_ref[...] = whitened_ref[...]
    overall = jnp.sum(all_ref[...], axis=0)
    enrichment_ref[...] = group_ref[0] * chroms / overall


def local(panel, zscores, block_chrom, lr_partner):
    samples, width = panel.shape
    owners = lax.axis_size("genome")
    chroms = lax.axis_size("chrom")
    tiles = samples // TILE
    share = len(tile_order(tiles)) * TILE // owners
    packed_shape = jax.ShapeDtypeStruct((owners, share + META, TILE), jnp.bfloat16)
    params = pltpu.CompilerParams(vmem_limit_bytes=48 * 2**20)

    lr_hbm, panel_hbm, z_hbm = (
        pltpu.with_memory_space_constraint(x, pltpu.HBM) for x in (lr_partner, panel, zscores.reshape(1, width))
    )
    packed, scores = pl.pallas_call(
        functools.partial(gram_kernel, owners, share),
        out_shape=(packed_shape, jax.ShapeDtypeStruct((1, width), jnp.float32)),
        in_specs=[HBM, SMEM, HBM, HBM],
        out_specs=(VMEM, VMEM),
        scratch_shapes=[
            pltpu.VMEM(panel.shape, panel.dtype),
            pltpu.SMEM(lr_partner.shape, jnp.int32),
            pltpu.SemaphoreType.DMA((tiles // 2 + 2,)),
        ],
        compiler_params=params,
    )(lr_hbm, block_chrom, panel_hbm, z_hbm)
    held = lax.all_to_all(packed, "genome", 0, 0, tiled=True)

    mixed, diagonals = pl.pallas_call(
        mix_kernel,
        out_shape=(
            jax.ShapeDtypeStruct((owners, share, TILE), jnp.bfloat16),
            jax.ShapeDtypeStruct((owners, META, TILE), jnp.float32),
        ),
        in_specs=[VMEM],
        out_specs=(VMEM, VMEM),
        compiler_params=params,
    )(held)
    sums = lax.all_to_all(mixed, "genome", 0, 0, tiled=True)

    whitened, totals = pl.pallas_call(
        functools.partial(finish_kernel, share),
        out_shape=(
            jax.ShapeDtypeStruct((1, width), jnp.float32),
            jax.ShapeDtypeStruct((owners, 1, TILE), jnp.float32),
        ),
        in_specs=[VMEM] * 4,
        out_specs=(VMEM, VMEM),
        scratch_shapes=[
            pltpu.VMEM((samples, samples), jnp.bfloat16),
            pltpu.VMEM((width, width), jnp.float32),
            pltpu.VMEM((width, width), jnp.float32),
        ],
        compiler_params=params,
    )(sums, diagonals, panel, scores)

    of_group = lax.all_to_all(totals, "genome", 0, 0, tiled=True)
    group_sum = jnp.sum(of_group, axis=0, keepdims=True)
    of_all = lax.all_to_all(
        jnp.broadcast_to(group_sum, (chroms, 1, TILE)), "chrom", 0, 0, tiled=True
    )
    whitened, enrichment = pl.pallas_call(
        functools.partial(close_kernel, chroms),
        out_shape=(
            jax.ShapeDtypeStruct((1, width), jnp.float32),
            jax.ShapeDtypeStruct((1, TILE), jnp.float32),
        ),
        in_specs=[VMEM] * 3,
        out_specs=(VMEM, VMEM),
        compiler_params=params,
    )(whitened, group_sum, of_all)
    return (whitened.reshape(width), enrichment.reshape(TILE)[:1])


def solution(mesh):
    placed = (
        P(None, ("chrom", "genome")),
        P(("chrom", "genome")),
        P(("chrom", "genome")),
        P(("chrom", "genome"), None),
    )
    return jax.shard_map(
        local,
        mesh=mesh,
        in_specs=placed,
        out_specs=(P(("chrom", "genome")), P("chrom")),
        check_vma=False,
    )
```

```python
import functools

import jax
import jax.numpy as jnp
from jax import lax
from jax.experimental import pallas as pl
from jax.experimental.pallas import tpu as pltpu
from jax.sharding import PartitionSpec as P

ridge_term = 0.5
leak_weight = 0.25

TILE = 128
SUB = 16
META = 8
META_P0, META_P1, META_HI, META_LO = 3, 4, 5, 6

NT = (((1,), (1,)), ((), ()))
VMEM = pl.BlockSpec(memory_space=pltpu.VMEM)
HBM = pl.BlockSpec(memory_space=pltpu.HBM)
SMEM = pl.BlockSpec(memory_space=pltpu.SMEM)


def tile_order(tiles):
    below = [(i, j) for j in range(tiles) for i in range(j + 1, tiles)]
    return below + [(2 * c, 2 * c) for c in range(tiles // 2)]


def grid_ids(shape):
    return lax.broadcasted_iota(jnp.int32, shape, 0), lax.broadcasted_iota(jnp.int32, shape, 1)


def pieces(start, share):
    out, row = [], 0
    while row < TILE:
        owner, place = divmod(start + row, share)
        length = min(TILE - row, share - place)
        out.append((row, owner, place, length))
        row += length
    return out


def gram_kernel(owners, share, partner_hbm, chrom_ref, panel_hbm, out_ref, panel_ref, partner_ref, sems):
    samples = panel_ref.shape[0]
    tiles = samples // TILE
    bands = tiles // 2
    arriving = []
    for c in range(bands):
        band = pl.ds(2 * c * TILE, 2 * TILE)
        arriving.append(pltpu.make_async_copy(panel_hbm.at[band], panel_ref.at[band], sems.at[c]))
    small = [
        pltpu.make_async_copy(partner_hbm, partner_ref, sems.at[bands]),
    ]
    for copy in arriving + small:
        copy.start()
    order = {tile: n for n, tile in enumerate(tile_order(tiles))}
    rows, cols = grid_ids((TILE, TILE))
    metas = []

    def put(tile, value):
        value = value.astype(jnp.bfloat16)
        for row, owner, place, length in pieces(order[tile] * TILE, share):
            out_ref[owner, place : place + length, :] = value[row : row + length, :]

    for copy in arriving:
        copy.wait()
    for c in range(bands):
        low = 2 * c * TILE
        product = lax.dot_general(
            panel_ref[low:, :], panel_ref[low : low + 2 * TILE, :], NT, preferred_element_type=jnp.float32
        )
        for j in (2 * c, 2 * c + 1):
            for i in range(j + 1, tiles):
                put((i, j), product[i * TILE - low : (i + 1) * TILE - low, (j - 2 * c) * TILE : (j - 2 * c + 1) * TILE])
        first, second = product[:TILE, :TILE], product[TILE : 2 * TILE, TILE:]
        halved = jnp.where(rows == cols, 0.5 * second, second)
        put((2 * c, 2 * c), jnp.where(rows > cols, first, halved))
        metas.append((c, jnp.sum(jnp.where(rows == cols, 0.5 * first, 0.0), axis=0, keepdims=True)))

    owner_rows, _ = grid_ids((META, TILE))
    meta = jnp.zeros((META, TILE), jnp.float32)
    for n, diagonal in metas:
        meta = jnp.where(owner_rows == n, diagonal, meta)
    for copy in small:
        copy.wait()
    chrom = chrom_ref[0]
    for n, number in (
        (META_P0, lax.rem(partner_ref[0, 0], owners)),
        (META_P1, lax.rem(partner_ref[0, 1], owners)),
        (META_HI, chrom >> 4),
        (META_LO, chrom & 15),
    ):
        meta = jnp.where(owner_rows == n, number.astype(jnp.float32), meta)
    meta = meta.astype(jnp.bfloat16)
    for owner in range(owners):
        out_ref[owner, share : share + META, :] = meta


def mix_kernel(in_ref, out_ref, diagonal_ref):
    owners, height, _ = in_ref.shape
    share = height - META
    meta = in_ref[:, share:, :].astype(jnp.float32)

    def spread(n):
        return jnp.broadcast_to(meta[:, n : n + 1, :], (owners, SUB, TILE))

    def flat(value):
        return value.reshape(owners * SUB, TILE)

    high, low = spread(META_HI), spread(META_LO)
    same = jnp.where(
        (high[1:] == high[:-1]) & (low[1:] == low[:-1]), 1.0, 0.0
    )
    edge = jnp.zeros((1, SUB, TILE), jnp.float32)
    with_right = flat(jnp.concatenate([same, edge], axis=0))
    with_left = flat(jnp.concatenate([edge, same], axis=0))
    first, second = flat(spread(META_P0)), flat(spread(META_P1))
    rows, cols = grid_ids((owners * SUB, TILE))
    own = (rows // SUB).astype(jnp.float32)
    halves = []
    for h in range(owners * SUB // TILE):
        other = (cols // SUB + h * (TILE // SUB)).astype(jnp.float32)
        count = jnp.where(first == other, 1.0, 0.0) + jnp.where(second == other, 1.0, 0.0)
        count = count + jnp.where(own + 1.0 == other, with_right, 0.0) + jnp.where(own - 1.0 == other, with_left, 0.0)
        halves.append(jnp.where(rows % SUB == cols % SUB, count, 0.0))
    weights = jnp.concatenate(halves, axis=1).astype(jnp.bfloat16)

    groups = share // SUB
    for g in range(0, groups, 2):
        members = list(range(g, min(g + 2, groups)))
        stacked = jnp.concatenate(
            [in_ref[:, m * SUB : (m + 1) * SUB, :].reshape(owners * SUB, TILE) for m in members], axis=1
        )
        mixed = jnp.dot(weights, stacked, preferred_element_type=jnp.float32).astype(jnp.bfloat16)
        for n, m in enumerate(members):
            out_ref[:, m * SUB : (m + 1) * SUB, :] = mixed[:, n * TILE : (n + 1) * TILE].reshape(owners, SUB, TILE)
    padded = jnp.concatenate([meta, jnp.zeros((owners, SUB - META, TILE), jnp.float32)], axis=1)
    mixed = jnp.dot(
        weights, padded.reshape(owners * SUB, TILE).astype(jnp.bfloat16), preferred_element_type=jnp.float32
    )
    diagonal_ref[...] = mixed.reshape(owners, SUB, TILE)[:, :META, :]


def finish_kernel(share, sums_ref, diagonal_ref, panel_ref, z_hbm, out_ref, total_ref, half, whole, shifted, z_ref, sem):
    arriving = pltpu.make_async_copy(z_hbm, z_ref, sem)
    arriving.start()
    samples, width = panel_ref.shape
    tiles = samples // TILE
    order = {tile: n for n, tile in enumerate(tile_order(tiles))}
    rows, cols = grid_ids((TILE, TILE))
    zero = jnp.zeros((TILE, TILE), jnp.bfloat16)

    def get(tile):
        return jnp.concatenate(
            [
                sums_ref[owner, place : place + length, :]
                for _, owner, place, length in pieces(order[tile] * TILE, share)
            ],
            axis=0,
        )

    def place(i, j, value):
        half[i * TILE : (i + 1) * TILE, j * TILE : (j + 1) * TILE] = value

    meta = diagonal_ref[lax.axis_index("genome")]
    for c in range(tiles // 2):
        for j in (2 * c, 2 * c + 1):
            for i in range(j + 1, tiles):
                place(i, j, get((i, j)))
        packed = get((2 * c, 2 * c)).astype(jnp.float32)
        lower = jnp.where(rows > cols, packed, jnp.where(rows == cols, meta[c : c + 1, :], 0.0))
        place(2 * c, 2 * c, lower.astype(jnp.bfloat16))
        place(2 * c + 1, 2 * c + 1, jnp.where(rows <= cols, packed, 0.0).astype(jnp.bfloat16))
        place(2 * c, 2 * c + 1, zero)

    parts = []
    for c in range(tiles // 2):
        low, top = 2 * c * TILE, (2 * c + 2) * TILE
        parts.append(
            jnp.dot(half[low:top, :top], panel_ref[:top, :], preferred_element_type=jnp.float32)
            * (leak_weight / samples)
            + 0.5 * panel_ref[low:top, :].astype(jnp.float32)
        )
    weighted = jnp.concatenate(parts, axis=0).astype(jnp.bfloat16)
    product = jnp.concatenate(
        [
            lax.dot_general(
                panel_ref[:, k : k + 2 * TILE], weighted, (((0,), (0,)), ((), ())), preferred_element_type=jnp.float32
            )
            for k in range(0, width, 2 * TILE)
        ],
        axis=0,
    )
    wide = width // TILE
    eye = rows == cols
    ridge = jnp.where(eye, ridge_term * samples, 0.0)
    both = product + product.T

    def with_ridge(m):
        own, above = m * TILE, (m + 1) * TILE
        band = both[own:above]
        return jnp.concatenate([band[:, :own], band[:, own:above] + ridge, band[:, above:]][(m == 0):(2 if m == wide - 1 else 3)], axis=1)

    matrix = jnp.concatenate([with_ridge(m) for m in range(wide)], axis=0)
    whole[...] = matrix
    shifted[...] = matrix
    norm = jnp.sqrt(jnp.sum(matrix * matrix, keepdims=True) + 1e-06 * samples * samples)
    inverse = 1.0 / norm
    for n in range(wide):
        own = slice(n * TILE, (n + 1) * TILE)
        shifted[own, own] = whole[own, own] - jnp.where(eye, 3.0 * norm, 0.0)

    def to_column(ref, row):
        return jnp.sum(ref[...] * row, axis=1, keepdims=True)

    def to_row(ref, column):
        return jnp.sum(ref[...] * column, axis=0, keepdims=True)

    def turned_column(column):
        return jnp.concatenate(
            [
                jnp.sum(jnp.where(eye, column[n * TILE : (n + 1) * TILE], 0.0), axis=0, keepdims=True)
                for n in range(wide)
            ],
            axis=1,
        )

    def turned_row(row):
        return jnp.concatenate(
            [
                jnp.sum(jnp.where(eye, row[:, n * TILE : (n + 1) * TILE], 0.0), axis=1, keepdims=True)
                for n in range(wide)
            ],
            axis=0,
        )

    def second_iterate(column, factor):
        inner = to_row(whole, column) * inverse
        inner = to_row(shifted, to_column(shifted, inner)) * (0.25 * inverse * inverse)
        return to_column(shifted, (3.0 * turned_column(column) - inner) * ((-0.25 * factor) * inverse))

    arriving.wait()
    z_row = z_ref[...]
    product = second_iterate(second_iterate(to_column(whole, z_row * inverse), 1.0), 1.0)
    answer = second_iterate(3.0 * turned_row(z_row) - product, 0.5)
    answer = turned_column(answer)
    out_ref[...] = answer
    total_ref[...] = jnp.broadcast_to(jnp.sum(answer * answer, keepdims=True).reshape(1, 1, 1), total_ref.shape)


def close_kernel(chroms, whitened_ref, group_ref, all_ref, out_ref, enrichment_ref):
    out_ref[...] = whitened_ref[...]
    overall = jnp.sum(all_ref[...], axis=0)
    enrichment_ref[...] = group_ref[0] * chroms / overall


def local(panel, zscores, block_chrom, lr_partner):
    samples, width = panel.shape
    owners = lax.axis_size("genome")
    chroms = lax.axis_size("chrom")
    tiles = samples // TILE
    share = len(tile_order(tiles)) * TILE // owners
    packed_shape = jax.ShapeDtypeStruct((owners, share + META, TILE), jnp.bfloat16)
    params = pltpu.CompilerParams(vmem_limit_bytes=48 * 2**20)

    lr_hbm, panel_hbm = (pltpu.with_memory_space_constraint(x, pltpu.HBM) for x in (lr_partner, panel))
    packed = pl.pallas_call(
        functools.partial(gram_kernel, owners, share),
        out_shape=packed_shape,
        in_specs=[HBM, SMEM, HBM],
        out_specs=VMEM,
        scratch_shapes=[
            pltpu.VMEM(panel.shape, panel.dtype),
            pltpu.SMEM(lr_partner.shape, jnp.int32),
            pltpu.SemaphoreType.DMA((tiles // 2 + 1,)),
        ],
        compiler_params=params,
    )(lr_hbm, block_chrom, panel_hbm)
    held = lax.all_to_all(packed, "genome", 0, 0, tiled=True)

    mixed, diagonals = pl.pallas_call(
        mix_kernel,
        out_shape=(
            jax.ShapeDtypeStruct((owners, share, TILE), jnp.bfloat16),
            jax.ShapeDtypeStruct((owners, META, TILE), jnp.float32),
        ),
        in_specs=[VMEM],
        out_specs=(VMEM, VMEM),
        compiler_params=params,
    )(held)
    sums = lax.all_to_all(mixed, "genome", 0, 0, tiled=True)

    whitened, totals = pl.pallas_call(
        functools.partial(finish_kernel, share),
        out_shape=(
            jax.ShapeDtypeStruct((1, width), jnp.float32),
            jax.ShapeDtypeStruct((owners, 1, TILE), jnp.float32),
        ),
        in_specs=[VMEM, VMEM, VMEM, HBM],
        out_specs=(VMEM, VMEM),
        scratch_shapes=[
            pltpu.VMEM((samples, samples), jnp.bfloat16),
            pltpu.VMEM((width, width), jnp.float32),
            pltpu.VMEM((width, width), jnp.float32),
            pltpu.VMEM((1, width), jnp.float32),
            pltpu.SemaphoreType.DMA,
        ],
        compiler_params=params,
    )(sums, diagonals, panel, pltpu.with_memory_space_constraint(zscores.reshape(1, width), pltpu.HBM))

    of_group = lax.all_to_all(totals, "genome", 0, 0, tiled=True)
    group_sum = jnp.sum(of_group, axis=0, keepdims=True)
    of_all = lax.all_to_all(
        jnp.broadcast_to(group_sum, (chroms, 1, TILE)), "chrom", 0, 0, tiled=True
    )
    whitened, enrichment = pl.pallas_call(
        functools.partial(close_kernel, chroms),
        out_shape=(
            jax.ShapeDtypeStruct((1, width), jnp.float32),
            jax.ShapeDtypeStruct((1, TILE), jnp.float32),
        ),
        in_specs=[VMEM] * 3,
        out_specs=(VMEM, VMEM),
        compiler_params=params,
    )(whitened, group_sum, of_all)
    return (whitened.reshape(width), enrichment.reshape(TILE)[:1])


def solution(mesh):
    placed = (
        P(None, ("chrom", "genome")),
        P(("chrom", "genome")),
        P(("chrom", "genome")),
        P(("chrom", "genome"), None),
    )
    return jax.shard_map(
        local,
        mesh=mesh,
        in_specs=placed,
        out_specs=(P(("chrom", "genome")), P("chrom")),
        check_vma=False,
    )
```
